32 devices in a mesh: gx: 4 (over z), gy: 8 (over y, x, core).
Axes of the slice: x: 2, y: 2, z: 4, core: 2. Of those that a mesh axis runs over, the one named last changes fastest.
Arguments:
- start_block: float32 [4, 8, 64, 16, 128], P('gx', 'gy')
- tiles: float32 [4, 8, 64, 4, 128, 128], P('gx', 'gy'), may hold values from -0.15625 to 0.15625
- tile_cols: int32 [4, 8, 64, 4], P('gx', 'gy'), may hold values from 0 to 63
- node_diag: float32 [4, 8, 64, 128], P('gx', 'gy'), may hold values from 3 to 24
- face_tiles: float32 [4, 8, 2, 24, 128, 128], P('gx', 'gy'), may hold values from -0.15625 to 0.15625
- face_rows: int32 [4, 8, 4, 24], P('gx', 'gy'), may hold values from 0 to 63, as said below
- filter_bounds: float32 [2], replicated, may hold values from 8 to 30, as said below
Outputs:
- basis: float32 [4, 8, 64, 16, 128], P('gx', 'gy')
- projected: float32 [16, 16], replicated
The draws below stay inside these ranges and needn't reach their ends.
Inputs may be any that keep to these rules, and one draw needn't show every extreme that they name: `tile_cols`: each stored tile's column is a tile row of the same subdomain. `face_rows`: each of the four lists of a subdomain names 24 distinct tile rows. `filter_bounds`: entry 0 lies in 8 to 10 and entry 1 in 26 to 30.
All inputs are finite; a program needn't handle non-finite values.
Results may differ from the reference program's by a relative error of at most 0.0003.
Values sent between devices are 32-bit elements; how exact they have to be, the bound alone decides.
No kernel may reach another device: no remote copies, remote signals or barrier semaphores. Data moves between devices by JAX's collectives and lax.ppermute only.
A program may use at most 128 MiB of HBM per device.

```python
import math
import jax
import jax.numpy as jnp
from jax import lax

COLS = 16
TILE = 128
NB = 4
TROWS = 64
FROWS = 24
SUB_X = 4
SUB_Y = 8


def draw_start_block(key, part):
    key = jax.random.fold_in(key, 11)
    shape = (SUB_X, SUB_Y, TROWS, COLS, TILE)
    base = jax.random.normal(key, shape, jnp.float32)
    along_x = jnp.arange(SUB_X, dtype=jnp.float32)[:, None] / max(SUB_X - 1, 1)
    along_y = jnp.arange(SUB_Y, dtype=jnp.float32)[None, :] / max(SUB_Y - 1, 1)
    scale = 1.0 + along_x + along_y
    return base * scale[:, :, None, None, None]


def draw_face_rows(key, part):
    key = jax.random.fold_in(key, 23)
    scores = jax.random.randint(key, (SUB_X, SUB_Y, 4, TROWS), 0, 1 << 16, dtype=jnp.int32)
    scores = scores * TROWS + jnp.arange(TROWS, dtype=jnp.int32)
    order = jnp.argsort(scores, axis=-1, stable=True)
    return order[..., :FROWS].astype(jnp.int32)


def draw_filter_bounds(key, part):
    key = jax.random.fold_in(key, 37)
    shares = jax.random.uniform(key, (2,), jnp.float32)
    return jnp.array([8.0, 26.0], jnp.float32) + shares * jnp.array([2.0, 4.0], jnp.float32)


def plant(values, stream_key, smallest, largest):
    longest = values.shape.index(max(values.shape))
    spots = []
    for shift in (0, 1):
        where = [jax.random.randint(jax.random.fold_in(stream_key, axis), (), 0, length) for axis, length in enumerate(values.shape)]
        where[longest] = (where[longest] + shift) % values.shape[longest]
        spots.append(tuple(where))
    return values.at[spots[0]].set(smallest).at[spots[1]].set(largest)


def block_levels(key, extent, shards, smallest, top_value):
    factor_of, own = 1.0, jax.random.fold_in(key, 6)
    for dim, blocks in shards:
        draws = jnp.exp(jax.random.uniform(jax.random.fold_in(own, dim), (blocks,), jnp.float32, smallest / len(shards), top_value / len(shards)))
        factor_of = factor_of * jnp.repeat(draws, extent[dim] // blocks).reshape([-1 if axis == dim else 1 for axis in range(len(extent))])
    return factor_of


def noise(own_key, extent, scale, reach, pieces=(), kind=jnp.bfloat16):
    drawn = scale * jax.random.normal(own_key, extent, jnp.float32)
    if pieces:
        drawn = drawn * block_levels(own_key, extent, pieces, -0.22, 0.18)
    return jnp.clip(drawn, -reach, reach).astype(kind)


def setup_inputs(seed: int = 0) -> dict:
    arg_keys = jax.random.split(jax.random.key(seed), 8)
    return {
        "start_block": draw_start_block(jax.random.fold_in(arg_keys[7], 71), 0),
        "tiles": noise(arg_keys[1], (SUB_X, SUB_Y, TROWS, NB, TILE, TILE), (2 * NB * TILE + 2 * TILE) ** -0.5, 0.15625, ((0, 4), (1, 8)), jnp.float32),
        "tile_cols": plant(jax.random.randint(arg_keys[2], (SUB_X, SUB_Y, TROWS, NB), 0, TROWS), jax.random.fold_in(arg_keys[2], 1), 0, TROWS - 1).astype(jnp.int32),
        "node_diag": jnp.clip(jnp.exp(math.log(24.0) - 2.0794415 * jax.random.uniform(arg_keys[3], (SUB_X, SUB_Y, TROWS, TILE), jnp.float32) ** block_levels(arg_keys[3], (SUB_X, SUB_Y, TROWS, TILE), ((0, 4), (1, 8)), -0.2, 0.2)), 3.0, 24.0),
        "face_tiles": noise(arg_keys[4], (SUB_X, SUB_Y, 2, FROWS, TILE, TILE), (2 * NB * TILE + 2 * TILE) ** -0.5, 0.15625, ((0, 4), (1, 8)), jnp.float32),
        "face_rows": draw_face_rows(jax.random.fold_in(arg_keys[7], 71), 0),
        "filter_bounds": draw_filter_bounds(jax.random.fold_in(arg_keys[7], 71), 0),
    }


HIGH = lax.Precision.HIGHEST

def local_apply(block, tiles, cols, diag):
    count = block.shape[0]
    gathered = block[cols]
    forward = jnp.einsum('rkcb,rkab->rca', gathered, tiles, precision=HIGH)
    terms = jnp.einsum('rca,rkab->rkcb', block, tiles, precision=HIGH)
    onehot = (cols.reshape(-1)[:, None] == jnp.arange(count, dtype=jnp.int32)[None, :]).astype(block.dtype)
    backward = jnp.einsum('mr,mcb->rcb', onehot, terms.reshape((-1,) + terms.shape[2:]), precision=HIGH)
    return diag[:, None, :] * block + forward + backward

def place(rows, data, count):
    onehot = (rows[:, None] == jnp.arange(count, dtype=jnp.int32)[None, :]).astype(data.dtype)
    return jnp.einsum('fr,fcn->rcn', onehot, data, precision=HIGH)

def face_terms(block, face_tiles, face_rows, axis):
    if axis == 0:
        plus_face, minus_face, which = (0, 1, 0)
    else:
        plus_face, minus_face, which = (2, 3, 1)
    count = block.shape[2]
    length = block.shape[axis]
    pick = jax.vmap(jax.vmap(lambda one, rows: one[rows]))
    minus = pick(block, face_rows[:, :, minus_face])
    plus = pick(block, face_rows[:, :, plus_face])
    coupling = face_tiles[:, :, which]
    upper = jnp.concatenate([lax.slice_in_dim(minus, 1, length, axis=axis), jnp.zeros_like(lax.slice_in_dim(minus, 0, 1, axis=axis))], axis=axis)
    gain = jnp.einsum('uvfcb,uvfab->uvfca', upper, coupling, precision=HIGH)
    outgoing = jnp.einsum('uvfca,uvfab->uvfcb', plus, coupling, precision=HIGH)
    lower = jnp.concatenate([jnp.zeros_like(lax.slice_in_dim(outgoing, 0, 1, axis=axis)), lax.slice_in_dim(outgoing, 0, length - 1, axis=axis)], axis=axis)
    placer = jax.vmap(jax.vmap(lambda rows, data: place(rows, data, count)))
    return placer(face_rows[:, :, plus_face], gain) + placer(face_rows[:, :, minus_face], lower)

def reference(start_block, tiles, tile_cols, node_diag, face_tiles, face_rows, filter_bounds):

    def operate(block):
        total = jax.vmap(jax.vmap(local_apply))(block, tiles, tile_cols, node_diag)
        total = total + face_terms(block, face_tiles, face_rows, 0)
        return total + face_terms(block, face_tiles, face_rows, 1)
    half = (filter_bounds[1] - filter_bounds[0]) / 2.0
    centre = (filter_bounds[1] + filter_bounds[0]) / 2.0
    first = (operate(start_block) - centre * start_block) / half
    second = 2.0 * (operate(first) - centre * first) / half - start_block
    filtered = 2.0 * (operate(second) - centre * second) / half - first
    nodes = filtered.shape[0] * filtered.shape[1] * filtered.shape[2] * filtered.shape[4]
    gram = jnp.einsum('uvrcn,uvrdn->cd', filtered, filtered, precision=HIGH) / nodes
    factor = jnp.linalg.cholesky(gram)
    identity = jnp.eye(gram.shape[0], dtype=gram.dtype)
    inverse = lax.linalg.triangular_solve(factor, identity, left_side=True, lower=True)
    basis = jnp.einsum('cd,uvrdn->uvrcn', inverse, filtered, precision=HIGH)
    image = operate(basis)
    raw = jnp.einsum('uvrcn,uvrdn->cd', basis, image, precision=HIGH) / nodes
    projected = (raw + raw.T) / 2.0
    return (basis, projected)
```

```python
import functools

import jax
import jax.numpy as jnp
from jax import lax
from jax.experimental import pallas as pl
from jax.experimental.pallas import tpu as pltpu
from jax.sharding import PartitionSpec as P

F32 = jnp.float32
BF16 = jnp.bfloat16
MIB = 1 << 20
VM = pl.BlockSpec(memory_space=pltpu.VMEM)
SM = pl.BlockSpec(memory_space=pltpu.SMEM)
ANY = pl.BlockSpec(memory_space=pl.ANY)
cat = jnp.concatenate

ROWS = 8
SHRINK = 1.0 / 64.0


def split(x):
    high = x.astype(BF16)
    low = (x - high.astype(F32)).astype(BF16)
    return high, low


def stacked(x):
    return cat(split(x), axis=-2)


def dot_nn(x, t):
    return lax.dot_general(x, t, (((1,), (0,)), ((), ())), preferred_element_type=F32)


def dot_nt(x, t):
    return lax.dot_general(x, t, (((1,), (1,)), ((), ())), preferred_element_type=F32)


def fold(both, low=None):
    half = both.shape[0] // 2
    out = both[:half] + both[half:]
    return out if low is None else out + low


def two_piece(dot, x2, high, low):
    half = x2.shape[0] // 2
    return fold(dot(x2, high), dot(x2[:half], low))


def place_rows(w_ref, rows, which, data, j):
    at = rows[which, j]
    w_ref[at] = w_ref[at] + data


def leave(v_ref, v2_ref, rows, ch, cl, sends, products):
    faces = rows.shape[1]
    for axis in range(2):
        minus = sends[2 * axis]

        def copy(j, carry, axis=axis, minus=minus):
            minus[j] = v_ref[rows[2 * axis + 1, j]]
            return carry

        lax.fori_loop(0, faces, copy, 0, unroll=8)
    if not products:
        return

    def step(s, carry):
        outs = []
        for axis in range(2):
            for r in range(ROWS):
                j = s * ROWS + r
                x2 = v2_ref[rows[2 * axis, j]]
                outs.append((axis, j, two_piece(dot_nn, x2, ch[axis, j], cl[axis, j])))
        for axis, j, out in outs:
            sends[2 * axis + 1][j] = out
        return carry

    lax.fori_loop(0, faces // ROWS, step, 0)


def begin_kernel(rows, v, tiles, ch, cl, v2, mx, ox, my, oy):
    v2[...] = stacked(v[...])
    high, low = split(tiles[...])
    ch[...] = high
    cl[...] = low
    leave(v, v2, rows, ch, cl, (mx, ox, my, oy), True)


def local_rows(rows, cols, v2, highs, lows, wf, wb):
    outs = []
    for i, high, low in zip(rows, highs, lows):
        x2 = v2[i]
        g2 = cat([v2[cols[i, k]] for k in range(4)], axis=1)
        high = cat(high, axis=1)
        low = cat(low, axis=1)
        outs.append((two_piece(dot_nt, g2, high, low), two_piece(dot_nn, x2, high, low)))
    for i, (forward, backward) in zip(rows, outs):
        wf[i] = forward
        for k in range(4):
            at = cols[i, k]
            wb[at] = wb[at] + backward[:, k * 128 : (k + 1) * 128]


def first_kernel(cols, v2, tiles, wf, wb, th, tl, stage, sems):
    count = v2.shape[0]
    copies = count // ROWS

    def fetch(c):
        part = pl.ds(c * ROWS, ROWS)
        return pltpu.make_async_copy(tiles.at[part], stage.at[part], sems.at[c])

    for c in range(copies):
        fetch(c).start()
    wb[...] = jnp.zeros_like(wb)

    def step(c, carry):
        fetch(c).wait()
        rows, highs, lows = [], [], []
        for r in range(ROWS):
            i = c * ROWS + r
            pieces = [split(stage[i, k]) for k in range(4)]
            for k in range(4):
                th[i, k] = pieces[k][0]
                tl[i, k] = pieces[k][1]
            rows.append(i)
            highs.append([p[0] for p in pieces])
            lows.append([p[1] for p in pieces])
        local_rows(rows, cols, v2, highs, lows, wf, wb)
        return carry

    lax.fori_loop(0, copies, step, 0)


def local_kernel(cols, v2, th, tl, wf, wb):
    wb[...] = jnp.zeros_like(wb)

    def step(c, carry):
        rows = [c * ROWS + r for r in range(ROWS)]
        highs = [[th[i, k] for k in range(4)] for i in rows]
        lows = [[tl[i, k] for k in range(4)] for i in rows]
        local_rows(rows, cols, v2, highs, lows, wf, wb)
        return carry

    lax.fori_loop(0, v2.shape[0] // ROWS, step, 0)


def arrive(rows, flags, received, ch, cl, acc):
    faces = rows.shape[1]

    def step(s, carry):
        outs = []
        for axis in range(2):
            upper, lower = received[2 * axis], received[2 * axis + 1]
            for r in range(ROWS):
                j = s * ROWS + r
                u2 = stacked(jnp.where(flags[2 * axis] > 0, upper[j], 0.0))
                gain = two_piece(dot_nt, u2, ch[axis, j], cl[axis, j])
                outs.append((axis, j, gain, jnp.where(flags[2 * axis + 1] > 0, lower[j], 0.0)))
        for axis, j, gain, low in outs:
            place_rows(acc, rows, 2 * axis, gain, j)
            place_rows(acc, rows, 2 * axis + 1, low, j)
        return carry

    lax.fori_loop(0, faces // ROWS, step, 0)


def next_kernel(order, rows, flags, bounds, *refs):
    if order == 1:
        (v, wf, wb, diag, ux, lx, uy, ly, ch, cl, *outs, acc) = refs
        older = None
    else:
        (v, older, wf, wb, diag, ux, lx, uy, ly, ch, cl, *outs, acc) = refs
    new, new2, *sends = outs
    acc[...] = jnp.zeros_like(acc)
    arrive(rows, flags, (ux, lx, uy, ly), ch, cl, acc)
    lower = jnp.full((16, 128), bounds[0], F32)
    upper = jnp.full((16, 128), bounds[1], F32)
    half = (upper - lower) / 2.0
    centre = (upper + lower) / 2.0
    scale = (1.0 if order == 1 else 2.0) / half
    group = 8

    def step(s, carry):
        part = pl.ds(s * group, group)
        x = v[part]
        ax = wf[part] + wb[part] + acc[part] + diag[part][:, None, :] * x
        y = (ax - centre * x) * scale
        if older is not None:
            y = y - older[part]
        new[part] = y
        new2[part] = stacked(y)
        return carry

    lax.fori_loop(0, v.shape[0] // group, step, 0)
    if order < 3:
        leave(new, new2, rows, ch, cl, sends, True)
        return
    mx, my, gram = sends
    leave(new, new2, rows, ch, cl, (mx, None, my, None), False)
    total = jnp.zeros((32, 32), F32)
    for s in range(0, v.shape[0], 16):
        x2 = cat([new2[s + r] for r in range(16)], axis=1)
        total = total + dot_nt(x2, x2)
    spread(gram, quarter(total))


def quarter(total):
    half = total.shape[0] // 2
    return (total[:half, :half] + total[half:, half:]) + (total[:half, half:] + total[half:, :half])


def spread(out, value):
    def step(d, carry):
        out[d] = value
        return carry

    lax.fori_loop(0, out.shape[0], step, 0)


def project_kernel(cols, v, v2, diag, th, out, y2):
    def step(c, carry):
        outs = []
        for r in range(ROWS):
            i = c * ROWS + r
            g2 = cat([v2[cols[i, k]] for k in range(4)], axis=1)
            outs.append((i, fold(dot_nt(g2, cat([th[i, k] for k in range(4)], axis=1)))))
        for i, forward in outs:
            y2[i] = stacked((forward + 0.5 * (diag[pl.ds(i, 1)] * v[i])) * SHRINK)
        return carry

    lax.fori_loop(0, v.shape[0] // ROWS, step, 0)
    total = jnp.zeros((32, 32), F32)
    for s in range(0, v.shape[0], 16):
        a2 = cat([v2[s + r] for r in range(16)], axis=1)
        b2 = cat([y2[s + r] for r in range(16)], axis=1)
        total = total + dot_nt(a2, b2)
    out[...] = quarter(total)


def project_faces_kernel(rows, flags, v2, ux, uy, ch, part, out):
    total = jnp.zeros((32, 32), F32)
    for axis, upper in ((0, ux), (1, uy)):
        for s in range(0, rows.shape[1], ROWS):
            lefts, rights = [], []
            for r in range(ROWS):
                j = s + r
                u2 = stacked(jnp.where(flags[2 * axis] > 0, upper[j], 0.0))
                rights.append(stacked(fold(dot_nt(u2, ch[axis, j])) * SHRINK))
                lefts.append(v2[rows[2 * axis, j]])
            total = total + dot_nt(cat(lefts, axis=1), cat(rights, axis=1))
    spread(out, part[...] + quarter(total))


def summed(ref):
    total = ref[0]
    for d in range(1, ref.shape[0]):
        total = total + ref[d]
    return total


def basis_kernel(nodes, gram, v2, basis, inverse):
    g = summed(gram) / nodes
    n = g.shape[0]
    row = lax.broadcasted_iota(jnp.int32, (n, n), 0)
    col = lax.broadcasted_iota(jnp.int32, (n, n), 1)
    e = jnp.where(row == col, 1.0, 0.0).astype(F32)
    pivots = jnp.zeros((n, n), F32)
    for k in range(n):
        pivot = jnp.broadcast_to(g[k : k + 1, k : k + 1], (n, n))
        pivots = jnp.where(row == k, pivot, pivots)
        factor = jnp.broadcast_to(g[:, k : k + 1], (n, n)) / pivot
        factor = jnp.where(row > k, factor, 0.0)
        g = g - factor * g[k : k + 1, :]
        e = e - factor * e[k : k + 1, :]
    inv = e / jnp.sqrt(pivots)
    inverse[...] = inv
    high, low = split(inv)
    left = cat([cat([high, high], axis=1), cat([low, jnp.zeros_like(low)], axis=1)], axis=0)

    for s in range(0, v2.shape[0], 8):
        out = fold(dot_nn(left, cat([v2[s + r] for r in range(8)], axis=1)))
        for r in range(8):
            basis[s + r] = out[:, r * 128 : (r + 1) * 128]


def projected_kernel(nodes, sums, inverse, out):
    half = summed(sums)
    inv = inverse[...]
    high = lax.Precision.HIGHEST
    raw = lax.dot_general(inv, half, (((1,), (0,)), ((), ())), precision=high, preferred_element_type=F32)
    raw = lax.dot_general(raw, inv, (((1,), (1,)), ((), ())), precision=high, preferred_element_type=F32)
    out[...] = (raw + raw.T) * (1.0 / (SHRINK * nodes))


def in_vmem(shape, dtype):
    return pltpu.VMEM(shape, dtype)


def call(kernel, name, specs, outs, scratch=(), limit=32, flops=0, nbytes=0):
    return pl.pallas_call(
        kernel,
        name=name,
        in_specs=specs,
        out_specs=[VM] * len(outs),
        out_shape=outs,
        scratch_shapes=list(scratch),
        cost_estimate=pl.CostEstimate(flops=flops, bytes_accessed=nbytes, transcendentals=0),
        compiler_params=pltpu.CompilerParams(vmem_limit_bytes=limit * MIB),
    )


def ring(x, axis, by):
    peers = lax.axis_size(axis)
    return lax.ppermute(x, axis, [(i, (i + by) % peers) for i in range(peers)])


def shards(start_block, tiles, tile_cols, node_diag, face_tiles, face_rows, filter_bounds):
    block = start_block[0, 0]
    stored = tiles[0, 0]
    cols = tile_cols[0, 0]
    diag = node_diag[0, 0]
    coupling = face_tiles[0, 0]
    rows = face_rows[0, 0]
    count, width, tile = block.shape
    faces = rows.shape[1]
    nx, ny = lax.axis_size("gx"), lax.axis_size("gy")
    peers = nx * ny
    nodes = float(count * tile * peers)
    ix, iy = lax.axis_index("gx"), lax.axis_index("gy")
    flags = jnp.stack([ix < nx - 1, ix > 0, iy < ny - 1, iy > 0]).astype(jnp.int32)

    vec = in_vmem((count, width, tile), F32)
    vec2 = in_vmem((count, 2 * width, tile), BF16)
    face = jax.ShapeDtypeStruct((faces, width, tile), F32)
    tile2 = in_vmem(stored.shape, BF16)
    face2 = in_vmem(coupling.shape, BF16)
    small = jax.ShapeDtypeStruct((peers, width, width), F32)
    local_flops = 16 * stored.size * width

    ch, cl, x2, mx, ox, my, oy = call(
        begin_kernel, "begin", [SM, VM, VM], [face2, face2, vec2, face, face, face, face]
    )(rows, block, coupling)

    def exchange(mx, ox, my, oy):
        return (ring(mx, "gx", -1), ring(ox, "gx", 1), ring(my, "gy", -1), ring(oy, "gy", 1))

    received = exchange(mx, ox, my, oy)
    wf, wb, th, tl = call(
        first_kernel, "local_first", [SM, VM, ANY], [vec, vec, tile2, tile2],
        [pltpu.VMEM(stored.shape, F32), pltpu.SemaphoreType.DMA((count // ROWS,))],
        limit=40, flops=local_flops, nbytes=4 * stored.size,
    )(cols, x2, stored)

    x, older = block, None
    for order in (1, 2, 3):
        carried = (x,) if older is None else (x, older)
        last = order == 3
        outs = [vec, vec2] + ([face, face, small] if last else [face] * 4)
        new, new2, *sends = call(
            functools.partial(next_kernel, order), "finish%d" % order,
            [SM, SM, SM] + [VM] * (9 + len(carried)), outs,
            [pltpu.VMEM((count, width, tile), F32)],
        )(rows, flags, filter_bounds, *carried, wf, wb, diag, *received, ch, cl)
        x, x2, older = new, new2, x
        if not last:
            received = exchange(*sends)
            wf, wb = call(
                local_kernel, "local%d" % (order + 1), [SM] + [VM] * 3, [vec, vec],
                flops=local_flops, nbytes=4 * stored.size,
            )(cols, x2, th, tl)
    mx, my, gram = sends
    gram = lax.all_to_all(gram, ("gx", "gy"), 0, 0)
    ux, uy = ring(mx, "gx", -1), ring(my, "gy", -1)
    (part,) = call(
        project_kernel, "project", [SM] + [VM] * 4, [in_vmem((width, width), F32)],
        [pltpu.VMEM((count, 2 * width, tile), BF16)],
        flops=local_flops // 4, nbytes=2 * stored.size,
    )(cols, x, x2, diag, th)
    (sums,) = call(project_faces_kernel, "project_faces", [SM, SM] + [VM] * 5, [small])(
        rows, flags, x2, ux, uy, ch, part
    )
    sums = lax.all_to_all(sums, ("gx", "gy"), 0, 0)
    basis, inverse = call(
        functools.partial(basis_kernel, nodes), "basis", [VM, VM],
        [jax.ShapeDtypeStruct((count, width, tile), F32), in_vmem((width, width), F32)],
        flops=1 << 24, nbytes=MIB,
    )(gram, x2)
    (projected,) = call(
        functools.partial(projected_kernel, nodes), "projected", [VM, VM],
        [jax.ShapeDtypeStruct((width, width), F32)],
    )(sums, inverse)
    return (basis[None, None], projected)


def solution(mesh):
    in_specs = (
        P("gx", "gy", None, None, None),
        P("gx", "gy", None, None, None, None),
        P("gx", "gy", None, None),
        P("gx", "gy", None, None),
        P("gx", "gy", None, None, None, None),
        P("gx", "gy", None, None),
        P(),
    )
    out_specs = (P("gx", "gy", None, None, None), P())
    return jax.shard_map(shards, mesh=mesh, in_specs=in_specs, out_specs=out_specs, check_vma=False)
```

```python
import functools

import jax
import jax.numpy as jnp
from jax import lax
from jax.experimental import pallas as pl
from jax.experimental.pallas import tpu as pltpu
from jax.sharding import PartitionSpec as P

F32 = jnp.float32
BF16 = jnp.bfloat16
MIB = 1 << 20
VM = pl.BlockSpec(memory_space=pltpu.VMEM)
SM = pl.BlockSpec(memory_space=pltpu.SMEM)
HBM = pl.BlockSpec(memory_space=pltpu.HBM)
cat = jnp.concatenate

ROWS = 8
EARLY = 24
SHRINK = 1.0 / 64.0


def split(x):
    high = x.astype(BF16)
    low = (x - high.astype(F32)).astype(BF16)
    return high, low


def stacked(x):
    return cat(split(x), axis=-2)


def dot_nn(x, t):
    return lax.dot_general(x, t, (((1,), (0,)), ((), ())), preferred_element_type=F32)


def dot_nt(x, t):
    return lax.dot_general(x, t, (((1,), (1,)), ((), ())), preferred_element_type=F32)


def fold(both, low=None):
    half = both.shape[0] // 2
    out = both[:half] + both[half:]
    return out if low is None else out + low


def two_piece(dot, x2, high, low):
    half = x2.shape[0] // 2
    return fold(dot(x2, high), dot(x2[:half], low))


def place_rows(w_ref, rows, which, data, j):
    at = rows[which, j]
    w_ref[at] = w_ref[at] + data


def leave(v, v2, rows, flags, ch, cl, sends):
    def step(s, carry):
        outs = []
        for axis in range(2):
            for r in range(ROWS):
                j = s * ROWS + r
                x2 = v2[rows[2 * axis, j]]
                outs.append((axis, j, two_piece(dot_nn, x2, ch[axis, j], cl[axis, j])))
        for axis, j, out in outs:
            send(rows, flags, v, axis, j, out, sends)
        return carry

    lax.fori_loop(0, rows.shape[1] // ROWS, step, 0)


def begin_kernel(rows_in, cols_in, bounds_in, flags_in, block, tiles, stored, *refs):
    (rows, cols, bounds, flags, ch, cl, v, v2, a, b, c, d, early, stage, sems) = refs
    faces = rows.shape[1]
    chunks = faces // ROWS

    def fetch(s, axis):
        part = pl.ds(s * ROWS, ROWS)
        at = sems.at[2 * s + axis]
        return pltpu.make_async_copy(tiles.at[axis, part], stage.at[axis, part], at)

    def bring(source, target, k):
        copy = pltpu.make_async_copy(source, target, sems.at[2 * chunks + k])
        copy.start()
        return copy

    small = [bring(x, y, k) for k, (x, y) in enumerate(((rows_in, rows), (flags_in, flags), (block, v)))]
    for s in range(chunks):
        for axis in range(2):
            fetch(s, axis).start()
    late = [bring(cols_in, cols, 3), bring(bounds_in, bounds, 4)]
    late.append(bring(stored.at[pl.ds(0, EARLY)], early, 5))
    for copy in small:
        copy.wait()
    v2[...] = stacked(v[...])

    def step(s, carry):
        outs = []
        for axis in range(2):
            fetch(s, axis).wait()
            for r in range(ROWS):
                j = s * ROWS + r
                high, low = split(stage[axis, j])
                ch[axis, j] = high
                cl[axis, j] = low
                outs.append((axis, j, two_piece(dot_nn, v2[rows[2 * axis, j]], high, low)))
        for axis, j, out in outs:
            send(rows, flags, v, axis, j, out, (a, b, c, d))
        return carry

    lax.fori_loop(0, chunks, step, 0)
    for copy in late:
        copy.wait()


def send(rows, flags, v, axis, j, product, sends):
    minus = v[rows[2 * axis + 1, j]]
    odd = flags[4 + axis] > 0
    sends[2 * axis][j] = jnp.where(odd, minus, product)
    sends[2 * axis + 1][j] = jnp.where(odd, product, minus)


def local_rows(rows, cols, v2, highs, lows, wf, wb):
    outs = []
    for i, high, low in zip(rows, highs, lows):
        x2 = v2[i]
        g2 = cat([v2[cols[k, i]] for k in range(4)], axis=1)
        high = cat(high, axis=1)
        low = cat(low, axis=1)
        outs.append((two_piece(dot_nt, g2, high, low), two_piece(dot_nn, x2, high, low)))
    for i, (forward, backward) in zip(rows, outs):
        wf[i] = forward
        for k in range(4):
            at = cols[k, i]
            wb[at] = wb[at] + backward[:, k * 128 : (k + 1) * 128]


def first_kernel(cols, v2, early, tiles, wf, wb, th, tl, stage, sems):
    copies = stage.shape[0] // ROWS

    def fetch(c):
        part = pl.ds(c * ROWS, ROWS)
        return pltpu.make_async_copy(
            tiles.at[pl.ds(EARLY + c * ROWS, ROWS)], stage.at[part], sems.at[c]
        )

    for c in range(copies):
        fetch(c).start()
    wb[...] = jnp.zeros_like(wb)

    def work(source, start, c):
        rows, highs, lows = [], [], []
        for r in range(ROWS):
            i = start + c * ROWS + r
            pieces = [split(source[c * ROWS + r, k]) for k in range(4)]
            for k in range(4):
                th[i, k] = pieces[k][0]
                tl[i, k] = pieces[k][1]
            rows.append(i)
            highs.append([p[0] for p in pieces])
            lows.append([p[1] for p in pieces])
        local_rows(rows, cols, v2, highs, lows, wf, wb)

    def step_early(c, carry):
        work(early, 0, c)
        return carry

    def step(c, carry):
        fetch(c).wait()
        work(stage, EARLY, c)
        return carry

    lax.fori_loop(0, EARLY // ROWS, step_early, 0)
    lax.fori_loop(0, copies, step, 0)


def local_kernel(cols, v2, th, tl, wf, wb):
    wb[...] = jnp.zeros_like(wb)

    def step(c, carry):
        rows = [c * ROWS + r for r in range(ROWS)]
        highs = [[th[i, k] for k in range(4)] for i in rows]
        lows = [[tl[i, k] for k in range(4)] for i in rows]
        local_rows(rows, cols, v2, highs, lows, wf, wb)
        return carry

    lax.fori_loop(0, v2.shape[0] // ROWS, step, 0)


def arrive(rows, flags, received, ch, cl, acc):
    faces = rows.shape[1]

    def step(s, carry):
        outs = []
        for axis in range(2):
            odd = flags[4 + axis] > 0
            for r in range(ROWS):
                j = s * ROWS + r
                even, other = received[2 * axis][j], received[2 * axis + 1][j]
                u2 = stacked(jnp.where(flags[2 * axis] > 0, jnp.where(odd, other, even), 0.0))
                gain = two_piece(dot_nt, u2, ch[axis, j], cl[axis, j])
                outs.append((axis, j, gain, jnp.where(flags[2 * axis + 1] > 0, jnp.where(odd, even, other), 0.0)))
        for axis, j, gain, low in outs:
            place_rows(acc, rows, 2 * axis, gain, j)
            place_rows(acc, rows, 2 * axis + 1, low, j)
        return carry

    lax.fori_loop(0, faces // ROWS, step, 0)


def next_kernel(order, rows, flags, bounds, *refs):
    if order == 1:
        (v, wf, wb, diag, ux, lx, uy, ly, ch, cl, *outs, acc) = refs
        older = None
    else:
        (v, older, wf, wb, diag, ux, lx, uy, ly, ch, cl, *outs, acc) = refs
    new, new2, *sends = outs
    acc[...] = jnp.zeros_like(acc)
    arrive(rows, flags, (ux, lx, uy, ly), ch, cl, acc)
    lower = jnp.full((16, 128), bounds[0], F32)
    upper = jnp.full((16, 128), bounds[1], F32)
    half = (upper - lower) / 2.0
    centre = (upper + lower) / 2.0
    scale = (1.0 if order == 1 else 2.0) / half
    group = 8

    def step(s, carry):
        part = pl.ds(s * group, group)
        x = v[part]
        ax = wf[part] + wb[part] + acc[part] + diag[part][:, None, :] * x
        y = (ax - centre * x) * scale
        if older is not None:
            y = y - older[part]
        new[part] = y
        new2[part] = stacked(y)
        return carry

    lax.fori_loop(0, v.shape[0] // group, step, 0)
    if order < 3:
        leave(new, new2, rows, flags, ch, cl, sends)
        return
    mx, my, gram = sends

    def copy(j, carry):
        mx[j] = new[rows[1, j]]
        my[j] = new[rows[3, j]]
        return carry

    lax.fori_loop(0, rows.shape[1], copy, 0, unroll=8)
    total = jnp.zeros((32, 32), F32)
    for s in range(0, v.shape[0], 16):
        x2 = cat([new2[s + r] for r in range(16)], axis=1)
        total = total + dot_nt(x2, x2)
    gram[...] = quarter(total)


def quarter(total):
    half = total.shape[0] // 2
    return (total[:half, :half] + total[half:, half:]) + (total[:half, half:] + total[half:, :half])


def spread(out, gram, half):
    value = cat([gram[:8], gram[8:], half[:8], half[8:]], axis=1)
    value = cat([value, jnp.zeros((8, 128 - value.shape[1]), F32)], axis=1)

    def step(d, carry):
        out[d] = value
        return carry

    lax.fori_loop(0, out.shape[0], step, 0)


def project_kernel(cols, v, v2, diag, th, out, y2):
    def step(c, carry):
        outs = []
        for r in range(ROWS):
            i = c * ROWS + r
            g2 = cat([v2[cols[k, i]] for k in range(4)], axis=1)
            outs.append((i, fold(dot_nt(g2, cat([th[i, k] for k in range(4)], axis=1)))))
        for i, forward in outs:
            y2[i] = stacked((forward + 0.5 * (diag[pl.ds(i, 1)] * v[i])) * SHRINK)
        return carry

    lax.fori_loop(0, v.shape[0] // ROWS, step, 0)
    total = jnp.zeros((32, 32), F32)
    for s in range(0, v.shape[0], 16):
        a2 = cat([v2[s + r] for r in range(16)], axis=1)
        b2 = cat([y2[s + r] for r in range(16)], axis=1)
        total = total + dot_nt(a2, b2)
    out[...] = quarter(total)


def project_faces_kernel(rows, flags, v2, ux, uy, ch, part, gram, out):
    total = jnp.zeros((32, 32), F32)
    for axis, upper in ((0, ux), (1, uy)):
        for s in range(0, rows.shape[1], ROWS):
            lefts, rights = [], []
            for r in range(ROWS):
                j = s + r
                u2 = stacked(jnp.where(flags[2 * axis] > 0, upper[j], 0.0))
                rights.append(stacked(fold(dot_nt(u2, ch[axis, j])) * SHRINK))
                lefts.append(v2[rows[2 * axis, j]])
            total = total + dot_nt(cat(lefts, axis=1), cat(rights, axis=1))
    spread(out, gram[...], part[...] + quarter(total))


def end_kernel(nodes, sums, v2, basis, projected):
    total = sums[0]
    for d in range(1, sums.shape[0]):
        total = total + sums[d]
    n = v2.shape[1] // 2
    g = cat([total[:, :n], total[:, n : 2 * n]], axis=0) / nodes
    half = cat([total[:, 2 * n : 3 * n], total[:, 3 * n : 4 * n]], axis=0)
    row = lax.broadcasted_iota(jnp.int32, (n, n), 0)
    col = lax.broadcasted_iota(jnp.int32, (n, n), 1)
    e = jnp.where(row == col, 1.0, 0.0).astype(F32)
    pivots = jnp.zeros((n, n), F32)
    for k in range(n):
        pivot = jnp.broadcast_to(g[k : k + 1, k : k + 1], (n, n))
        pivots = jnp.where(row == k, pivot, pivots)
        factor = jnp.broadcast_to(g[:, k : k + 1], (n, n)) / pivot
        factor = jnp.where(row > k, factor, 0.0)
        g = g - factor * g[k : k + 1, :]
        e = e - factor * e[k : k + 1, :]
    inv = e / jnp.sqrt(pivots)
    high, low = split(inv)
    left = cat([cat([high, high], axis=1), cat([low, jnp.zeros_like(low)], axis=1)], axis=0)
    for s in range(0, v2.shape[0], 8):
        out = fold(dot_nn(left, cat([v2[s + r] for r in range(8)], axis=1)))
        for r in range(8):
            basis[s + r] = out[:, r * 128 : (r + 1) * 128]
    exact = dict(precision=lax.Precision.HIGHEST, preferred_element_type=F32)
    raw = lax.dot_general(inv, half, (((1,), (0,)), ((), ())), **exact)
    raw = lax.dot_general(raw, inv, (((1,), (1,)), ((), ())), **exact)
    projected[...] = (raw + raw.T) * (1.0 / (SHRINK * nodes))


def in_hbm(x):
    return pltpu.with_memory_space_constraint(x, pltpu.HBM)


def in_vmem(shape, dtype):
    return pltpu.VMEM(shape, dtype)


def call(kernel, name, specs, outs, scratch=(), limit=6, flops=0, nbytes=0, smem=0):
    return pl.pallas_call(
        kernel,
        name=name,
        in_specs=specs,
        out_specs=[SM] * smem + [VM] * (len(outs) - smem),
        out_shape=outs,
        scratch_shapes=list(scratch),
        cost_estimate=pl.CostEstimate(flops=flops, bytes_accessed=nbytes, transcendentals=0),
        compiler_params=pltpu.CompilerParams(vmem_limit_bytes=limit * MIB),
    )


def ring(x, axis, by):
    peers = lax.axis_size(axis)
    return lax.ppermute(x, axis, [(i, (i + by) % peers) for i in range(peers)])


def pairs(x, axis, odd):
    nx, ny = lax.axis_size("gx"), lax.axis_size("gy")
    moves = []
    for u in range(nx):
        for w in range(ny):
            at, size = (u, nx) if axis == 0 else (w, ny)
            if odd and at in (0, size - 1):
                to = (u, w ^ 1) if axis == 0 else (u ^ 1, w)
            else:
                other = at + 1 if at % 2 == odd else at - 1
                to = (other, w) if axis == 0 else (u, other)
            moves.append((u * ny + w, to[0] * ny + to[1]))
    return lax.ppermute(x, ("gx", "gy"), moves)


def shards(start_block, tiles, tile_cols, node_diag, face_tiles, face_rows, filter_bounds):
    block = start_block[0, 0]
    stored = tiles[0, 0]
    cols = tile_cols[0, 0].T
    diag = node_diag[0, 0]
    coupling = face_tiles[0, 0]
    rows = face_rows[0, 0]
    count, width, tile = block.shape
    faces = rows.shape[1]
    nx, ny = lax.axis_size("gx"), lax.axis_size("gy")
    peers = nx * ny
    nodes = float(count * tile * peers)
    ix, iy = lax.axis_index("gx"), lax.axis_index("gy")
    flags = jnp.stack(
        [ix < nx - 1, ix > 0, iy < ny - 1, iy > 0, ix % 2 == 1, iy % 2 == 1]
    ).astype(jnp.int32)

    vec = in_vmem((count, width, tile), F32)
    vec2 = in_vmem((count, 2 * width, tile), BF16)
    face = jax.ShapeDtypeStruct((faces, width, tile), F32)
    tile2 = in_vmem(stored.shape, BF16)
    face2 = in_vmem(coupling.shape, BF16)
    square = in_vmem((width, width), F32)
    small = jax.ShapeDtypeStruct((peers, 8, 128), F32)
    local_flops = 16 * stored.size * width

    rows, cols, filter_bounds, flags, ch, cl, block, x2, *sends, early = call(
        begin_kernel, "begin", [HBM] * 7,
        [
            pltpu.SMEM(rows.shape, jnp.int32), pltpu.SMEM(cols.shape, jnp.int32),
            pltpu.SMEM((2,), F32), pltpu.SMEM(flags.shape, jnp.int32),
            face2, face2, vec, vec2, face, face, face, face,
            in_vmem((EARLY,) + stored.shape[1:], F32),
        ],
        [pltpu.VMEM(coupling.shape, F32), pltpu.SemaphoreType.DMA((2 * (faces // ROWS) + 6,))],
        limit=6, flops=local_flops // 2, nbytes=4 * stored.size // 2, smem=4,
    )(*(in_hbm(x) for x in (rows, cols, filter_bounds, flags, block, coupling, stored)))

    def exchange(sends):
        return tuple(pairs(x, k // 2, k % 2) for k, x in enumerate(sends))

    received = exchange(sends)
    wf, wb, th, tl = call(
        first_kernel, "local_first", [SM, VM, VM, HBM], [vec, vec, tile2, tile2],
        [
            pltpu.VMEM((count - EARLY,) + stored.shape[1:], F32),
            pltpu.SemaphoreType.DMA(((count - EARLY) // ROWS,)),
        ],
        limit=14, flops=local_flops, nbytes=4 * stored.size,
    )(cols, x2, early, in_hbm(stored))

    x, older = block, None
    for order in (1, 2, 3):
        carried = (x,) if older is None else (x, older)
        last = order == 3
        outs = [vec, vec2] + ([face, face, square] if last else [face] * 4)
        new, new2, *sends = call(
            functools.partial(next_kernel, order), "finish%d" % order,
            [SM, SM, SM] + [VM] * (9 + len(carried)), outs,
            [pltpu.VMEM((count, width, tile), F32)],
        )(rows, flags, filter_bounds, *carried, wf, wb, diag, *received, ch, cl)
        x, x2, older = new, new2, x
        if not last:
            received = exchange(sends)
            wf, wb = call(
                local_kernel, "local%d" % (order + 1), [SM] + [VM] * 3, [vec, vec],
                flops=local_flops, nbytes=4 * stored.size,
            )(cols, x2, th, tl)
    mx, my, gram = sends
    ux, uy = ring(mx, "gx", -1), ring(my, "gy", -1)
    (part,) = call(
        project_kernel, "project", [SM] + [VM] * 4, [square],
        [pltpu.VMEM((count, 2 * width, tile), BF16)],
        flops=local_flops // 4, nbytes=2 * stored.size,
    )(cols, x, x2, diag, th)
    (sums,) = call(project_faces_kernel, "project_faces", [SM, SM] + [VM] * 6, [small])(
        rows, flags, x2, ux, uy, ch, part, gram
    )
    sums = lax.all_to_all(sums, ("gx", "gy"), 0, 0)
    basis, projected = call(
        functools.partial(end_kernel, nodes), "end", [VM, VM],
        [jax.ShapeDtypeStruct((count, width, tile), F32), jax.ShapeDtypeStruct((width, width), F32)],
    )(sums, x2)
    return (basis[None, None], projected)


def solution(mesh):
    in_specs = (
        P("gx", "gy", None, None, None),
        P("gx", "gy", None, None, None, None),
        P("gx", "gy", None, None),
        P("gx", "gy", None, None),
        P("gx", "gy", None, None, None, None),
        P("gx", "gy", None, None),
        P(),
    )
    out_specs = (P("gx", "gy", None, None, None), P())
    return jax.shard_map(shards, mesh=mesh, in_specs=in_specs, out_specs=out_specs, check_vma=False)
```

```python
import functools

import jax
import jax.numpy as jnp
from jax import lax
from jax.experimental import pallas as pl
from jax.experimental.pallas import tpu as pltpu
from jax.sharding import PartitionSpec as P

F32 = jnp.float32
BF16 = jnp.bfloat16
MIB = 1 << 20
VM = pl.BlockSpec(memory_space=pltpu.VMEM)
SM = pl.BlockSpec(memory_space=pltpu.SMEM)
HBM = pl.BlockSpec(memory_space=pltpu.HBM)
cat = jnp.concatenate

ROWS = 8
FACES = 24
EARLY = 16
SHRINK = 1.0 / 64.0


def split(x):
    high = x.astype(BF16)
    low = (x - high.astype(F32)).astype(BF16)
    return high, low


def stacked(x):
    return cat(split(x), axis=-2)


def dot_nn(x, t):
    return lax.dot_general(x, t, (((1,), (0,)), ((), ())), preferred_element_type=F32)


def dot_nt(x, t):
    return lax.dot_general(x, t, (((1,), (1,)), ((), ())), preferred_element_type=F32)


def fold(both, low=None):
    half = both.shape[0] // 2
    out = both[:half] + both[half:]
    return out if low is None else out + low


def two_piece(dot, x2, high, low):
    half = x2.shape[0] // 2
    return fold(dot(x2, high), dot(x2[:half], low))


def place_rows(w_ref, rows, which, data, j):
    at = rows[which, j]
    w_ref[at] = w_ref[at] + data


def leave(v, v2, rows, flags, ch, cl, sends):
    def step(s, carry):
        outs = []
        for axis in range(2):
            for r in range(FACES):
                j = s * FACES + r
                x2 = v2[rows[2 * axis, j]]
                outs.append((axis, j, two_piece(dot_nn, x2, ch[axis, j], cl[axis, j])))
        for axis, j, out in outs:
            send(rows, flags, v, axis, j, out, sends)
        return carry

    lax.fori_loop(0, rows.shape[1] // FACES, step, 0)


def begin_kernel(rows_in, cols_in, bounds_in, block, tiles, stored, *refs):
    (rows, cols, bounds, flags, ch, cl, v, v2, a, b, c, d, early, stage, sems) = refs
    faces = rows.shape[1]
    chunks = faces // ROWS

    def fetch(s, axis):
        part = pl.ds(s * ROWS, ROWS)
        at = sems.at[2 * s + axis]
        return pltpu.make_async_copy(tiles.at[axis, part], stage.at[axis, part], at)

    def bring(source, target, k):
        copy = pltpu.make_async_copy(source, target, sems.at[2 * chunks + k])
        copy.start()
        return copy

    small = [bring(x, y, k) for k, (x, y) in enumerate(((rows_in, rows), (block, v)))]
    for s in range(chunks):
        for axis in range(2):
            fetch(s, axis).start()
    nx, ny = lax.axis_size("gx"), lax.axis_size("gy")
    ix, iy = lax.axis_index("gx"), lax.axis_index("gy")
    for k, flag in enumerate((ix < nx - 1, ix > 0, iy < ny - 1, iy > 0, ix % 2 == 1, iy % 2 == 1)):
        flags[k] = flag.astype(jnp.int32)
    late = [bring(cols_in, cols, 3), bring(bounds_in, bounds, 4)]
    late.append(bring(stored.at[pl.ds(0, EARLY)], early, 5))
    for copy in small:
        copy.wait()
    v2[...] = stacked(v[...])

    def step(s, carry):
        outs = []
        for axis in range(2):
            fetch(s, axis).wait()
            for r in range(ROWS):
                j = s * ROWS + r
                high, low = split(stage[axis, j])
                ch[axis, j] = high
                cl[axis, j] = low
                outs.append((axis, j, two_piece(dot_nn, v2[rows[2 * axis, j]], high, low)))
        for axis, j, out in outs:
            send(rows, flags, v, axis, j, out, (a, b, c, d))
        return carry

    lax.fori_loop(0, chunks, step, 0)
    for copy in late:
        copy.wait()


def send(rows, flags, v, axis, j, product, sends):
    minus = v[rows[2 * axis + 1, j]]
    odd = flags[4 + axis] > 0
    sends[2 * axis][j] = jnp.where(odd, minus, product)
    sends[2 * axis + 1][j] = jnp.where(odd, product, minus)


def local_rows(rows, cols, v2, highs, lows, wf, wb):
    outs = []
    for i, high, low in zip(rows, highs, lows):
        x2 = v2[i]
        g2 = cat([v2[cols[k, i]] for k in range(4)], axis=1)
        high = cat(high, axis=1)
        low = cat(low, axis=1)
        outs.append((two_piece(dot_nt, g2, high, low), two_piece(dot_nn, x2, high, low)))
    for i, (forward, backward) in zip(rows, outs):
        wf[i] = forward
        for k in range(4):
            at = cols[k, i]
            wb[at] = wb[at] + backward[:, k * 128 : (k + 1) * 128]


def first_kernel(cols, v2, early, tiles, wf, wb, th, tl, stage, sems):
    copies = stage.shape[0] // ROWS

    def fetch(c):
        part = pl.ds(c * ROWS, ROWS)
        return pltpu.make_async_copy(
            tiles.at[pl.ds(EARLY + c * ROWS, ROWS)], stage.at[part], sems.at[c]
        )

    for c in range(copies):
        fetch(c).start()
    wb[...] = jnp.zeros_like(wb)

    def work(source, start, c):
        rows, highs, lows = [], [], []
        for r in range(ROWS):
            i = start + c * ROWS + r
            pieces = [split(source[c * ROWS + r, k]) for k in range(4)]
            for k in range(4):
                th[i, k] = pieces[k][0]
                tl[i, k] = pieces[k][1]
            rows.append(i)
            highs.append([p[0] for p in pieces])
            lows.append([p[1] for p in pieces])
        local_rows(rows, cols, v2, highs, lows, wf, wb)

    def step_early(c, carry):
        work(early, 0, c)
        return carry

    def step(c, carry):
        fetch(c).wait()
        work(stage, EARLY, c)
        return carry

    lax.fori_loop(0, EARLY // ROWS, step_early, 0)
    lax.fori_loop(0, copies, step, 0)


def local_kernel(cols, v2, th, tl, wf, wb):
    wb[...] = jnp.zeros_like(wb)

    def step(c, carry):
        rows = [c * ROWS + r for r in range(ROWS)]
        highs = [[th[i, k] for k in range(4)] for i in rows]
        lows = [[tl[i, k] for k in range(4)] for i in rows]
        local_rows(rows, cols, v2, highs, lows, wf, wb)
        return carry

    lax.fori_loop(0, v2.shape[0] // ROWS, step, 0)


def arrive(rows, flags, received, ch, cl, acc):
    faces = rows.shape[1]

    def step(s, carry):
        outs = []
        for axis in range(2):
            odd = flags[4 + axis] > 0
            for r in range(FACES):
                j = s * FACES + r
                even, other = received[2 * axis][j], received[2 * axis + 1][j]
                u2 = stacked(jnp.where(flags[2 * axis] > 0, jnp.where(odd, other, even), 0.0))
                gain = two_piece(dot_nt, u2, ch[axis, j], cl[axis, j])
                outs.append((axis, j, gain, jnp.where(flags[2 * axis + 1] > 0, jnp.where(odd, even, other), 0.0)))
        for axis, j, gain, low in outs:
            place_rows(acc, rows, 2 * axis, gain, j)
            place_rows(acc, rows, 2 * axis + 1, low, j)
        return carry

    lax.fori_loop(0, faces // FACES, step, 0)


def next_kernel(order, rows, flags, bounds, *refs):
    if order == 1:
        (v, wf, wb, diag, ux, lx, uy, ly, ch, cl, *outs, acc) = refs
        older = None
    else:
        (v, older, wf, wb, diag, ux, lx, uy, ly, ch, cl, *outs, acc) = refs
    new, new2, *sends = outs
    acc[...] = jnp.zeros_like(acc)
    arrive(rows, flags, (ux, lx, uy, ly), ch, cl, acc)
    lower = jnp.full((16, 128), bounds[0], F32)
    upper = jnp.full((16, 128), bounds[1], F32)
    half = (upper - lower) / 2.0
    centre = (upper + lower) / 2.0
    scale = (1.0 if order == 1 else 2.0) / half
    group = 8

    def step(s, carry):
        part = pl.ds(s * group, group)
        x = v[part]
        ax = wf[part] + wb[part] + acc[part] + diag[part][:, None, :] * x
        y = (ax - centre * x) * scale
        if older is not None:
            y = y - older[part]
        new[part] = y
        new2[part] = stacked(y)
        return carry

    lax.fori_loop(0, v.shape[0] // group, step, 0)
    if order < 3:
        leave(new, new2, rows, flags, ch, cl, sends)
        return
    mx, my, gram = sends

    def copy(j, carry):
        mx[j] = new[rows[1, j]]
        my[j] = new[rows[3, j]]
        return carry

    lax.fori_loop(0, rows.shape[1], copy, 0, unroll=8)
    total = jnp.zeros((32, 32), F32)
    for s in range(0, v.shape[0], 16):
        x2 = cat([new2[s + r] for r in range(16)], axis=1)
        total = total + dot_nt(x2, x2)
    gram[...] = quarter(total)


def quarter(total):
    half = total.shape[0] // 2
    return (total[:half, :half] + total[half:, half:]) + (total[:half, half:] + total[half:, :half])


def spread(out, gram, half):
    value = cat([gram[:8], gram[8:], half[:8], half[8:]], axis=1)
    value = cat([value, jnp.zeros((8, 128 - value.shape[1]), F32)], axis=1)

    def step(d, carry):
        out[d] = value
        return carry

    lax.fori_loop(0, out.shape[0], step, 0)


def project_kernel(cols, v, v2, diag, th, out, wb):
    group = 8

    def begin(s, carry):
        part = pl.ds(s * group, group)
        wb[part] = 0.5 * (diag[part][:, None, :] * v[part])
        return carry

    lax.fori_loop(0, v.shape[0] // group, begin, 0)

    def step(c, carry):
        outs = []
        for r in range(ROWS):
            i = c * ROWS + r
            outs.append((i, fold(dot_nn(v2[i], cat([th[i, k] for k in range(4)], axis=1)))))
        for i, backward in outs:
            for k in range(4):
                at = cols[k, i]
                wb[at] = wb[at] + backward[:, k * 128 : (k + 1) * 128]
        return carry

    lax.fori_loop(0, v.shape[0] // ROWS, step, 0)
    total = jnp.zeros((32, 32), F32)
    for s in range(0, v.shape[0], 16):
        a2 = cat([v2[s + r] for r in range(16)], axis=1)
        b2 = cat([stacked(wb[s + r] * SHRINK) for r in range(16)], axis=1)
        total = total + dot_nt(a2, b2)
    out[...] = quarter(total)


def project_faces_kernel(rows, flags, v2, ux, uy, ch, part, gram, out):
    total = jnp.zeros((32, 32), F32)
    for axis, upper in ((0, ux), (1, uy)):
        for s in range(0, rows.shape[1], ROWS):
            lefts, rights = [], []
            for r in range(ROWS):
                j = s + r
                u2 = stacked(jnp.where(flags[2 * axis] > 0, upper[j], 0.0))
                rights.append(stacked(fold(dot_nt(u2, ch[axis, j])) * SHRINK))
                lefts.append(v2[rows[2 * axis, j]])
            total = total + dot_nt(cat(lefts, axis=1), cat(rights, axis=1))
    spread(out, gram[...], part[...] + quarter(total))


def end_kernel(nodes, sums, v2, basis, projected):
    total = sums[0]
    for d in range(1, sums.shape[0]):
        total = total + sums[d]
    n = v2.shape[1] // 2
    g = cat([total[:, :n], total[:, n : 2 * n]], axis=0) / nodes
    half = cat([total[:, 2 * n : 3 * n], total[:, 3 * n : 4 * n]], axis=0)
    row = lax.broadcasted_iota(jnp.int32, (n, n), 0)
    col = lax.broadcasted_iota(jnp.int32, (n, n), 1)
    e = jnp.where(row == col, 1.0, 0.0).astype(F32)
    pivots = jnp.zeros((n, n), F32)
    for k in range(n):
        pivot = jnp.broadcast_to(g[k : k + 1, k : k + 1], (n, n))
        pivots = jnp.where(row == k, pivot, pivots)
        factor = jnp.broadcast_to(g[:, k : k + 1], (n, n)) / pivot
        factor = jnp.where(row > k, factor, 0.0)
        g = g - factor * g[k : k + 1, :]
        e = e - factor * e[k : k + 1, :]
    inv = e / jnp.sqrt(pivots)
    high, low = split(inv)
    left = cat([cat([high, high], axis=1), cat([low, jnp.zeros_like(low)], axis=1)], axis=0)
    for s in range(0, v2.shape[0], 8):
        out = fold(dot_nn(left, cat([v2[s + r] for r in range(8)], axis=1)))
        for r in range(8):
            basis[s + r] = out[:, r * 128 : (r + 1) * 128]
    exact = dict(precision=lax.Precision.HIGHEST, preferred_element_type=F32)
    raw = lax.dot_general(inv, half, (((1,), (0,)), ((), ())), **exact)
    raw = lax.dot_general(raw, inv, (((1,), (1,)), ((), ())), **exact)
    projected[...] = (raw + raw.T) * (1.0 / (SHRINK * nodes))


def in_hbm(x):
    return pltpu.with_memory_space_constraint(x, pltpu.HBM)


def in_vmem(shape, dtype):
    return pltpu.VMEM(shape, dtype)


def call(kernel, name, specs, outs, scratch=(), limit=6, flops=0, nbytes=0, smem=0):
    return pl.pallas_call(
        kernel,
        name=name,
        in_specs=specs,
        out_specs=[SM] * smem + [VM] * (len(outs) - smem),
        out_shape=outs,
        scratch_shapes=list(scratch),
        cost_estimate=pl.CostEstimate(flops=flops, bytes_accessed=nbytes, transcendentals=0),
        compiler_params=pltpu.CompilerParams(vmem_limit_bytes=limit * MIB),
    )


def ring(x, axis, by):
    peers = lax.axis_size(axis)
    return lax.ppermute(x, axis, [(i, (i + by) % peers) for i in range(peers)])


def pairs(x, axis, odd):
    nx, ny = lax.axis_size("gx"), lax.axis_size("gy")
    moves = []
    for u in range(nx):
        for w in range(ny):
            at, size = (u, nx) if axis == 0 else (w, ny)
            if odd and at in (0, size - 1):
                to = (u, w ^ 1) if axis == 0 else (u ^ 1, w)
            else:
                other = at + 1 if at % 2 == odd else at - 1
                to = (other, w) if axis == 0 else (u, other)
            moves.append((u * ny + w, to[0] * ny + to[1]))
    return lax.ppermute(x, ("gx", "gy"), moves)


def shards(start_block, tiles, tile_cols, node_diag, face_tiles, face_rows, filter_bounds):
    block = start_block[0, 0]
    stored = tiles[0, 0]
    cols = tile_cols[0, 0].T
    diag = node_diag[0, 0]
    coupling = face_tiles[0, 0]
    rows = face_rows[0, 0]
    count, width, tile = block.shape
    faces = rows.shape[1]
    nx, ny = lax.axis_size("gx"), lax.axis_size("gy")
    peers = nx * ny
    nodes = float(count * tile * peers)
    vec = in_vmem((count, width, tile), F32)
    vec2 = in_vmem((count, 2 * width, tile), BF16)
    face = jax.ShapeDtypeStruct((faces, width, tile), F32)
    tile2 = in_vmem(stored.shape, BF16)
    face2 = in_vmem(coupling.shape, BF16)
    square = in_vmem((width, width), F32)
    small = jax.ShapeDtypeStruct((peers, 8, 128), F32)
    local_flops = 16 * stored.size * width

    rows, cols, filter_bounds, flags, ch, cl, block, x2, *sends, early = call(
        begin_kernel, "begin", [HBM] * 6,
        [
            pltpu.SMEM(rows.shape, jnp.int32), pltpu.SMEM(cols.shape, jnp.int32),
            pltpu.SMEM((2,), F32), pltpu.SMEM((6,), jnp.int32),
            face2, face2, vec, vec2, face, face, face, face,
            in_vmem((EARLY,) + stored.shape[1:], F32),
        ],
        [pltpu.VMEM(coupling.shape, F32), pltpu.SemaphoreType.DMA((2 * (faces // ROWS) + 6,))],
        limit=6, flops=local_flops // 2, nbytes=4 * stored.size // 2, smem=4,
    )(*(in_hbm(x) for x in (rows, cols, filter_bounds, block, coupling, stored)))

    def exchange(sends):
        return tuple(pairs(x, k // 2, k % 2) for k, x in enumerate(sends))

    received = exchange(sends)
    wf, wb, th, tl = call(
        first_kernel, "local_first", [SM, VM, VM, HBM], [vec, vec, tile2, tile2],
        [
            pltpu.VMEM((count - EARLY,) + stored.shape[1:], F32),
            pltpu.SemaphoreType.DMA(((count - EARLY) // ROWS,)),
        ],
        limit=18, flops=local_flops, nbytes=4 * stored.size,
    )(cols, x2, early, in_hbm(stored))

    x, older = block, None
    for order in (1, 2, 3):
        carried = (x,) if older is None else (x, older)
        last = order == 3
        outs = [vec, vec2] + ([face, face, square] if last else [face] * 4)
        new, new2, *sends = call(
            functools.partial(next_kernel, order), "finish%d" % order,
            [SM, SM, SM] + [VM] * (9 + len(carried)), outs,
            [pltpu.VMEM((count, width, tile), F32)],
        )(rows, flags, filter_bounds, *carried, wf, wb, diag, *received, ch, cl)
        x, x2, older = new, new2, x
        if not last:
            received = exchange(sends)
            wf, wb = call(
                local_kernel, "local%d" % (order + 1), [SM] + [VM] * 3, [vec, vec],
                flops=local_flops, nbytes=4 * stored.size,
            )(cols, x2, th, tl)
    mx, my, gram = sends
    ux, uy = ring(mx, "gx", -1), ring(my, "gy", -1)
    (part,) = call(
        project_kernel, "project", [SM] + [VM] * 4, [square],
        [pltpu.VMEM((count, width, tile), F32)],
        flops=local_flops // 4, nbytes=2 * stored.size,
    )(cols, x, x2, diag, th)
    (sums,) = call(project_faces_kernel, "project_faces", [SM, SM] + [VM] * 6, [small])(
        rows, flags, x2, ux, uy, ch, part, gram
    )
    sums = lax.all_to_all(sums, ("gx", "gy"), 0, 0)
    basis, projected = call(
        functools.partial(end_kernel, nodes), "end", [VM, VM],
        [jax.ShapeDtypeStruct((count, width, tile), F32), jax.ShapeDtypeStruct((width, width), F32)],
    )(sums, x2)
    return (basis[None, None], projected)


def solution(mesh):
    in_specs = (
        P("gx", "gy", None, None, None),
        P("gx", "gy", None, None, None, None),
        P("gx", "gy", None, None),
        P("gx", "gy", None, None),
        P("gx", "gy", None, None, None, None),
        P("gx", "gy", None, None),
        P(),
    )
    out_specs = (P("gx", "gy", None, None, None), P())
    return jax.shard_map(shards, mesh=mesh, in_specs=in_specs, out_specs=out_specs, check_vma=False)
```

```python
import functools

import jax
import jax.numpy as jnp
from jax import lax
from jax.experimental import pallas as pl
from jax.experimental.pallas import tpu as pltpu
from jax.sharding import PartitionSpec as P

F32 = jnp.float32
BF16 = jnp.bfloat16
F8 = jnp.float8_e4m3fn
MIB = 1 << 20
VM = pl.BlockSpec(memory_space=pltpu.VMEM)
SM = pl.BlockSpec(memory_space=pltpu.SMEM)
HBM = pl.BlockSpec(memory_space=pltpu.HBM)
cat = jnp.concatenate

ROWS = 8
FACES = 24
WIDE = 32
CHUNK = 8
EARLY = 16
TILE_SCALE = 2.0**19
VEC_SCALE = 256.0
SHRINK = 1.0 / 64.0


def split(x):
    high = x.astype(BF16)
    low = (x - high.astype(F32)).astype(BF16)
    return high, low


def low_tile(t, high):
    return ((t - high.astype(F32)) * TILE_SCALE).astype(F8)


def stacked8(x):
    high = x.astype(F8)
    low = (x - high.astype(F32)).astype(F8)
    return cat([high, low], axis=-2)


def vector_scales(peak):
    top = jnp.maximum(jnp.max(peak, axis=1, keepdims=True), 1e-30)
    top = jnp.broadcast_to(top, peak.shape)
    return VEC_SCALE / top, top * (1.0 / (VEC_SCALE * TILE_SCALE))


def shrunk(v, v8, peak, undo):
    up, down = vector_scales(peak)
    undo[...] = down
    group = 8

    def step(s, carry):
        part = pl.ds(s * group, group)
        v8[part] = stacked8(v[part] * up)
        return carry

    lax.fori_loop(0, v.shape[0] // group, step, 0)


def stacked(x):
    return cat(split(x), axis=-2)


def dot_nn(x, t):
    return lax.dot_general(x, t, (((1,), (0,)), ((), ())), preferred_element_type=F32)


def dot_nt(x, t):
    return lax.dot_general(x, t, (((1,), (1,)), ((), ())), preferred_element_type=F32)


def fold(both, low=None):
    half = both.shape[0] // 2
    out = both[:half] + both[half:]
    return out if low is None else out + low


def two_piece(dot, x2, high, low):
    half = x2.shape[0] // 2
    return fold(dot(x2, high), dot(x2[:half], low))


def place_rows(w_ref, rows, which, data, j):
    at = rows[which, j]
    w_ref[at] = w_ref[at] + data


def leave(v, v2, rows, flags, ch, cl, sends):
    def step(s, carry):
        outs = []
        for axis in range(2):
            for r in range(FACES):
                j = s * FACES + r
                x2 = v2[rows[2 * axis, j]]
                outs.append((axis, j, two_piece(dot_nn, x2, ch[axis, j], cl[axis, j])))
        for axis, j, out in outs:
            send(rows, flags, v, axis, j, out, sends)
        return carry

    lax.fori_loop(0, rows.shape[1] // FACES, step, 0)


def begin_kernel(rows_in, cols_in, bounds_in, block, tiles, stored, *refs):
    (rows, cols, bounds, flags, ch, cl, v, v2, v8, undo, a, b, c, d, early, stage, sems) = refs
    faces = rows.shape[1]
    chunks = faces // CHUNK

    def fetch(s, axis):
        part = pl.ds(s * CHUNK, CHUNK)
        at = sems.at[2 * s + axis]
        return pltpu.make_async_copy(tiles.at[axis, part], stage.at[axis, part], at)

    def bring(source, target, k):
        copy = pltpu.make_async_copy(source, target, sems.at[2 * chunks + k])
        copy.start()
        return copy

    small = [bring(x, y, k) for k, (x, y) in enumerate(((rows_in, rows), (block, v)))]
    for s in range(chunks):
        for axis in range(2):
            fetch(s, axis).start()
    nx, ny = lax.axis_size("gx"), lax.axis_size("gy")
    ix, iy = lax.axis_index("gx"), lax.axis_index("gy")
    for k, flag in enumerate((ix < nx - 1, ix > 0, iy < ny - 1, iy > 0, ix % 2 == 1, iy % 2 == 1)):
        flags[k] = flag.astype(jnp.int32)
    late = [bring(cols_in, cols, 3), bring(bounds_in, bounds, 4)]
    late.append(bring(stored.at[pl.ds(0, EARLY)], early, 5))
    for copy in small:
        copy.wait()
    v2[...] = stacked(v[...])
    shrunk(v, v8, jnp.max(jnp.abs(v[...]), axis=0), undo)

    def step(s, carry):
        outs = []
        for axis in range(2):
            fetch(s, axis).wait()
            for r in range(CHUNK):
                j = s * CHUNK + r
                high, low = split(stage[axis, j])
                ch[axis, j] = high
                cl[axis, j] = low
                outs.append((axis, j, two_piece(dot_nn, v2[rows[2 * axis, j]], high, low)))
        for axis, j, out in outs:
            send(rows, flags, v, axis, j, out, (a, b, c, d))
        return carry

    lax.fori_loop(0, chunks, step, 0)
    for copy in late:
        copy.wait()


def send(rows, flags, v, axis, j, product, sends):
    minus = v[rows[2 * axis + 1, j]]
    odd = flags[4 + axis] > 0
    sends[2 * axis][j] = jnp.where(odd, minus, product)
    sends[2 * axis + 1][j] = jnp.where(odd, product, minus)


def local_rows(rows, cols, v2, v8, undo, highs, lows, wf, wb):
    down = undo[...]
    wide = cat([down] * 4, axis=1)
    outs = []
    for i, high, low in zip(rows, highs, lows):
        at = [cols[k, i] for k in range(4)]
        high = cat(high, axis=1)
        low = cat(low, axis=1)
        forward = fold(dot_nt(cat([v2[c] for c in at], axis=1), high))
        forward = forward + down * fold(dot_nt(cat([v8[c] for c in at], axis=1), low))
        backward = fold(dot_nn(v2[i], high)) + wide * fold(dot_nn(v8[i], low))
        outs.append((forward, backward))
    for i, (forward, backward) in zip(rows, outs):
        wf[i] = forward
        for k in range(4):
            at = cols[k, i]
            wb[at] = wb[at] + backward[:, k * 128 : (k + 1) * 128]


def first_kernel(cols, v2, v8, undo, early, tiles, wf, wb, th, tl, stage, sems):
    copies = stage.shape[0] // ROWS

    def fetch(c):
        part = pl.ds(c * ROWS, ROWS)
        return pltpu.make_async_copy(
            tiles.at[pl.ds(EARLY + c * ROWS, ROWS)], stage.at[part], sems.at[c]
        )

    for c in range(copies):
        fetch(c).start()
    wb[...] = jnp.zeros_like(wb)

    def work(source, start, c):
        rows, highs, lows = [], [], []
        for r in range(ROWS):
            i = start + c * ROWS + r
            pieces = []
            for k in range(4):
                t = source[c * ROWS + r, k]
                high = t.astype(BF16)
                pieces.append((high, low_tile(t, high)))
            for k in range(4):
                th[i, k] = pieces[k][0]
                tl[i, k] = pieces[k][1]
            rows.append(i)
            highs.append([p[0] for p in pieces])
            lows.append([p[1] for p in pieces])
        local_rows(rows, cols, v2, v8, undo, highs, lows, wf, wb)

    def step_early(c, carry):
        work(early, 0, c)
        return carry

    def step(c, carry):
        fetch(c).wait()
        work(stage, EARLY, c)
        return carry

    lax.fori_loop(0, EARLY // ROWS, step_early, 0)
    lax.fori_loop(0, copies, step, 0)


def local_kernel(cols, v2, v8, undo, th, tl, wf, wb):
    wb[...] = jnp.zeros_like(wb)

    def step(c, carry):
        rows = [c * WIDE + r for r in range(WIDE)]
        highs = [[th[i, k] for k in range(4)] for i in rows]
        lows = [[tl[i, k] for k in range(4)] for i in rows]
        local_rows(rows, cols, v2, v8, undo, highs, lows, wf, wb)
        return carry

    lax.fori_loop(0, v2.shape[0] // WIDE, step, 0)


def arrive(rows, flags, received, ch, cl, acc):
    faces = rows.shape[1]

    def step(s, carry):
        outs = []
        for axis in range(2):
            odd = flags[4 + axis] > 0
            for r in range(FACES):
                j = s * FACES + r
                even, other = received[2 * axis][j], received[2 * axis + 1][j]
                u2 = stacked(jnp.where(flags[2 * axis] > 0, jnp.where(odd, other, even), 0.0))
                gain = two_piece(dot_nt, u2, ch[axis, j], cl[axis, j])
                outs.append((axis, j, gain, jnp.where(flags[2 * axis + 1] > 0, jnp.where(odd, even, other), 0.0)))
        for axis, j, gain, low in outs:
            place_rows(acc, rows, 2 * axis, gain, j)
            place_rows(acc, rows, 2 * axis + 1, low, j)
        return carry

    lax.fori_loop(0, faces // FACES, step, 0)


def next_kernel(order, rows, flags, bounds, *refs):
    if order == 1:
        (v, wf, wb, diag, ux, lx, uy, ly, ch, cl, *outs, acc) = refs
        older = None
    else:
        (v, older, wf, wb, diag, ux, lx, uy, ly, ch, cl, *outs, acc) = refs
    if order < 3:
        new, new2, new8, undo, *sends = outs
    else:
        new, new2, *sends = outs
    acc[...] = jnp.zeros_like(acc)
    arrive(rows, flags, (ux, lx, uy, ly), ch, cl, acc)
    lower = jnp.full((16, 128), bounds[0], F32)
    upper = jnp.full((16, 128), bounds[1], F32)
    half = (upper - lower) / 2.0
    centre = (upper + lower) / 2.0
    scale = (1.0 if order == 1 else 2.0) / half
    group = 8

    def step(s, carry):
        part = pl.ds(s * group, group)
        x = v[part]
        ax = wf[part] + wb[part] + acc[part] + diag[part][:, None, :] * x
        y = (ax - centre * x) * scale
        if older is not None:
            y = y - older[part]
        new[part] = y
        new2[part] = stacked(y)
        return jnp.maximum(carry, jnp.max(jnp.abs(y), axis=0))

    peak = lax.fori_loop(0, v.shape[0] // group, step, jnp.zeros((16, 128), F32))
    if order < 3:
        shrunk(new, new8, peak, undo)
        leave(new, new2, rows, flags, ch, cl, sends)
        return
    mx, my, gram = sends

    def copy(j, carry):
        mx[j] = new[rows[1, j]]
        my[j] = new[rows[3, j]]
        return carry

    lax.fori_loop(0, rows.shape[1], copy, 0, unroll=8)
    total = jnp.zeros((32, 32), F32)
    for s in range(0, v.shape[0], 16):
        x2 = cat([new2[s + r] for r in range(16)], axis=1)
        total = total + dot_nt(x2, x2)
    gram[...] = quarter(total)


def quarter(total):
    half = total.shape[0] // 2
    return (total[:half, :half] + total[half:, half:]) + (total[:half, half:] + total[half:, :half])


def spread(out, gram, half):
    value = cat([gram[:8], gram[8:], half[:8], half[8:]], axis=1)
    value = cat([value, jnp.zeros((8, 128 - value.shape[1]), F32)], axis=1)

    def step(d, carry):
        out[d] = value
        return carry

    lax.fori_loop(0, out.shape[0], step, 0)


def project_kernel(cols, v, v2, diag, th, out, wb):
    group = 8

    def begin(s, carry):
        part = pl.ds(s * group, group)
        wb[part] = 0.5 * (diag[part][:, None, :] * v[part])
        return carry

    lax.fori_loop(0, v.shape[0] // group, begin, 0)

    def step(c, carry):
        outs = []
        for r in range(WIDE):
            i = c * WIDE + r
            outs.append((i, fold(dot_nn(v2[i], cat([th[i, k] for k in range(4)], axis=1)))))
        for i, backward in outs:
            for k in range(4):
                at = cols[k, i]
                wb[at] = wb[at] + backward[:, k * 128 : (k + 1) * 128]
        return carry

    lax.fori_loop(0, v.shape[0] // WIDE, step, 0)
    total = jnp.zeros((32, 32), F32)
    for s in range(0, v.shape[0], 16):
        a2 = cat([v2[s + r] for r in range(16)], axis=1)
        b2 = cat([stacked(wb[s + r] * SHRINK) for r in range(16)], axis=1)
        total = total + dot_nt(a2, b2)
    out[...] = quarter(total)


def project_faces_kernel(rows, flags, v2, ux, uy, ch, part, gram, out):
    total = jnp.zeros((32, 32), F32)
    for axis, upper in ((0, ux), (1, uy)):
        for s in range(0, rows.shape[1], CHUNK):
            lefts, rights = [], []
            for r in range(CHUNK):
                j = s + r
                u2 = stacked(jnp.where(flags[2 * axis] > 0, upper[j], 0.0))
                rights.append(stacked(fold(dot_nt(u2, ch[axis, j])) * SHRINK))
                lefts.append(v2[rows[2 * axis, j]])
            total = total + dot_nt(cat(lefts, axis=1), cat(rights, axis=1))
    spread(out, gram[...], part[...] + quarter(total))


def end_kernel(nodes, sums, v2, basis, projected):
    total = sums[0]
    for d in range(1, sums.shape[0]):
        total = total + sums[d]
    n = v2.shape[1] // 2
    g = cat([total[:, :n], total[:, n : 2 * n]], axis=0) / nodes
    half = cat([total[:, 2 * n : 3 * n], total[:, 3 * n : 4 * n]], axis=0)
    row = lax.broadcasted_iota(jnp.int32, (n, n), 0)
    col = lax.broadcasted_iota(jnp.int32, (n, n), 1)
    e = jnp.where(row == col, 1.0, 0.0).astype(F32)
    pivots = jnp.zeros((n, n), F32)
    for k in range(n):
        pivot = jnp.broadcast_to(g[k : k + 1, k : k + 1], (n, n))
        pivots = jnp.where(row == k, pivot, pivots)
        factor = jnp.broadcast_to(g[:, k : k + 1], (n, n)) / pivot
        factor = jnp.where(row > k, factor, 0.0)
        g = g - factor * g[k : k + 1, :]
        e = e - factor * e[k : k + 1, :]
    inv = e / jnp.sqrt(pivots)
    high, low = split(inv)
    left = cat([cat([high, high], axis=1), cat([low, jnp.zeros_like(low)], axis=1)], axis=0)
    for s in range(0, v2.shape[0], 8):
        out = fold(dot_nn(left, cat([v2[s + r] for r in range(8)], axis=1)))
        for r in range(8):
            basis[s + r] = out[:, r * 128 : (r + 1) * 128]
    exact = dict(precision=lax.Precision.HIGHEST, preferred_element_type=F32)
    raw = lax.dot_general(inv, half, (((1,), (0,)), ((), ())), **exact)
    raw = lax.dot_general(raw, inv, (((1,), (1,)), ((), ())), **exact)
    projected[...] = (raw + raw.T) * (1.0 / (SHRINK * nodes))


def in_hbm(x):
    return pltpu.with_memory_space_constraint(x, pltpu.HBM)


def in_vmem(shape, dtype):
    return pltpu.VMEM(shape, dtype)


def call(kernel, name, specs, outs, scratch=(), limit=12, flops=0, nbytes=0, smem=0):
    return pl.pallas_call(
        kernel,
        name=name,
        in_specs=specs,
        out_specs=[SM] * smem + [VM] * (len(outs) - smem),
        out_shape=outs,
        scratch_shapes=list(scratch),
        cost_estimate=pl.CostEstimate(flops=flops, bytes_accessed=nbytes, transcendentals=0),
        compiler_params=pltpu.CompilerParams(vmem_limit_bytes=limit * MIB),
    )


def ring(x, axis, by):
    peers = lax.axis_size(axis)
    return lax.ppermute(x, axis, [(i, (i + by) % peers) for i in range(peers)])


def pairs(x, axis, odd):
    nx, ny = lax.axis_size("gx"), lax.axis_size("gy")
    moves = []
    for u in range(nx):
        for w in range(ny):
            at, size = (u, nx) if axis == 0 else (w, ny)
            if odd and at in (0, size - 1):
                to = (u, w ^ 1) if axis == 0 else (u ^ 1, w)
            else:
                other = at + 1 if at % 2 == odd else at - 1
                to = (other, w) if axis == 0 else (u, other)
            moves.append((u * ny + w, to[0] * ny + to[1]))
    return lax.ppermute(x, ("gx", "gy"), moves)


def shards(start_block, tiles, tile_cols, node_diag, face_tiles, face_rows, filter_bounds):
    block = start_block[0, 0]
    stored = tiles[0, 0]
    cols = tile_cols[0, 0].T
    diag = node_diag[0, 0]
    coupling = face_tiles[0, 0]
    rows = face_rows[0, 0]
    count, width, tile = block.shape
    faces = rows.shape[1]
    nx, ny = lax.axis_size("gx"), lax.axis_size("gy")
    peers = nx * ny
    nodes = float(count * tile * peers)
    vec = in_vmem((count, width, tile), F32)
    vec2 = in_vmem((count, 2 * width, tile), BF16)
    vec8 = in_vmem((count, 2 * width, tile), F8)
    scale = in_vmem((width, tile), F32)
    face = jax.ShapeDtypeStruct((faces, width, tile), F32)
    high, low = in_vmem(stored.shape, BF16), in_vmem(stored.shape, F8)
    face2 = in_vmem(coupling.shape, BF16)
    square = in_vmem((width, width), F32)
    small = jax.ShapeDtypeStruct((peers, 8, 128), F32)
    local_flops = 16 * stored.size * width

    rows, cols, filter_bounds, flags, ch, cl, block, x2, x8, undo, *sends, early = call(
        begin_kernel, "begin", [HBM] * 6,
        [
            pltpu.SMEM(rows.shape, jnp.int32), pltpu.SMEM(cols.shape, jnp.int32),
            pltpu.SMEM((2,), F32), pltpu.SMEM((6,), jnp.int32),
            face2, face2, vec, vec2, vec8, scale, face, face, face, face,
            in_vmem((EARLY,) + stored.shape[1:], F32),
        ],
        [pltpu.VMEM(coupling.shape, F32), pltpu.SemaphoreType.DMA((2 * (faces // CHUNK) + 6,))],
        limit=8, flops=local_flops // 2, nbytes=4 * stored.size // 2, smem=4,
    )(*(in_hbm(x) for x in (rows, cols, filter_bounds, block, coupling, stored)))

    def exchange(sends):
        return tuple(pairs(x, k // 2, k % 2) for k, x in enumerate(sends))

    received = exchange(sends)
    wf, wb, th, tl = call(
        first_kernel, "local_first", [SM] + [VM] * 4 + [HBM], [vec, vec, high, low],
        [
            pltpu.VMEM((count - EARLY,) + stored.shape[1:], F32),
            pltpu.SemaphoreType.DMA(((count - EARLY) // ROWS,)),
        ],
        limit=24, flops=local_flops, nbytes=4 * stored.size,
    )(cols, x2, x8, undo, early, in_hbm(stored))

    x, older = block, None
    for order in (1, 2, 3):
        carried = (x,) if older is None else (x, older)
        last = order == 3
        outs = [vec, vec2] + ([face, face, square] if last else [vec8, scale] + [face] * 4)
        new, new2, *sends = call(
            functools.partial(next_kernel, order), "finish%d" % order,
            [SM, SM, SM] + [VM] * (9 + len(carried)), outs,
            [pltpu.VMEM((count, width, tile), F32)],
        )(rows, flags, filter_bounds, *carried, wf, wb, diag, *received, ch, cl)
        x, x2, older = new, new2, x
        if not last:
            x8, undo, *sends = sends
            received = exchange(sends)
            wf, wb = call(
                local_kernel, "local%d" % (order + 1), [SM] + [VM] * 5, [vec, vec],
                flops=local_flops, nbytes=4 * stored.size,
            )(cols, x2, x8, undo, th, tl)
    mx, my, gram = sends
    ux, uy = ring(mx, "gx", -1), ring(my, "gy", -1)
    (part,) = call(
        project_kernel, "project", [SM] + [VM] * 4, [square],
        [pltpu.VMEM((count, width, tile), F32)],
        flops=local_flops // 4, nbytes=2 * stored.size,
    )(cols, x, x2, diag, th)
    (sums,) = call(project_faces_kernel, "project_faces", [SM, SM] + [VM] * 6, [small])(
        rows, flags, x2, ux, uy, ch, part, gram
    )
    sums = lax.all_to_all(sums, ("gx", "gy"), 0, 0)
    basis, projected = call(
        functools.partial(end_kernel, nodes), "end", [VM, VM],
        [jax.ShapeDtypeStruct((count, width, tile), F32), jax.ShapeDtypeStruct((width, width), F32)],
    )(sums, x2)
    return (basis[None, None], projected)


def solution(mesh):
    in_specs = (
        P("gx", "gy", None, None, None),
        P("gx", "gy", None, None, None, None),
        P("gx", "gy", None, None),
        P("gx", "gy", None, None),
        P("gx", "gy", None, None, None, None),
        P("gx", "gy", None, None),
        P(),
    )
    out_specs = (P("gx", "gy", None, None, None), P())
    return jax.shard_map(shards, mesh=mesh, in_specs=in_specs, out_specs=out_specs, check_vma=False)
```

```python
import functools

import jax
import jax.numpy as jnp
from jax import lax
from jax.experimental import pallas as pl
from jax.experimental.pallas import tpu as pltpu
from jax.sharding import PartitionSpec as P

F32 = jnp.float32
BF16 = jnp.bfloat16
F8 = jnp.float8_e4m3fn
MIB = 1 << 20
VM = pl.BlockSpec(memory_space=pltpu.VMEM)
SM = pl.BlockSpec(memory_space=pltpu.SMEM)
HBM = pl.BlockSpec(memory_space=pltpu.HBM)
cat = jnp.concatenate

ROWS = 8
FACES = 24
WIDE = 32
CHUNK = 8
EARLY = 16
TILE_SCALE = 2.0**19
VEC_SCALE = 256.0
SHRINK = 1.0 / 64.0


def split(x):
    high = x.astype(BF16)
    low = (x - high.astype(F32)).astype(BF16)
    return high, low


def low_tile(t, high):
    return ((t - high.astype(F32)) * TILE_SCALE).astype(F8)


def stacked8(x):
    high = x.astype(F8)
    low = (x - high.astype(F32)).astype(F8)
    return cat([high, low], axis=-2)


def vector_scales(peak):
    top = jnp.maximum(jnp.max(peak, axis=1, keepdims=True), 1e-30)
    top = jnp.broadcast_to(top, peak.shape)
    return VEC_SCALE / top, top * (1.0 / (VEC_SCALE * TILE_SCALE))


def shrunk(v, v8, peak, undo):
    up, down = vector_scales(peak)
    undo[...] = down
    group = 8

    def step(s, carry):
        part = pl.ds(s * group, group)
        v8[part] = stacked8(v[part] * up)
        return carry

    lax.fori_loop(0, v.shape[0] // group, step, 0)


def stacked(x):
    return cat(split(x), axis=-2)


def dot_nn(x, t):
    return lax.dot_general(x, t, (((1,), (0,)), ((), ())), preferred_element_type=F32)


def dot_nt(x, t):
    return lax.dot_general(x, t, (((1,), (1,)), ((), ())), preferred_element_type=F32)


def fold(both, low=None):
    half = both.shape[0] // 2
    out = both[:half] + both[half:]
    return out if low is None else out + low


def two_piece(dot, x2, high, low):
    half = x2.shape[0] // 2
    return fold(dot(x2, high), dot(x2[:half], low))


def place_rows(w_ref, rows, which, data, j):
    at = rows[which, j]
    w_ref[at] = w_ref[at] + data


def leave(v, v2, rows, flags, ch, cl, sends):
    def step(s, carry):
        outs = []
        for axis in range(2):
            for r in range(FACES):
                j = s * FACES + r
                x2 = v2[rows[2 * axis, j]]
                outs.append((axis, j, two_piece(dot_nn, x2, ch[axis, j], cl[axis, j])))
        for axis, j, out in outs:
            send(rows, flags, v, axis, j, out, sends)
        return carry

    lax.fori_loop(0, rows.shape[1] // FACES, step, 0)


def begin_kernel(rows_in, cols_in, bounds_in, block, tiles, stored, *refs):
    (rows, cols, bounds, flags, ch, cl, dh, dl, v, v2, v8, undo, a, b, c, d, early, stage, sems) = refs
    faces = rows.shape[1]
    chunks = faces // CHUNK

    def fetch(s, axis):
        part = pl.ds(s * CHUNK, CHUNK)
        at = sems.at[2 * s + axis]
        return pltpu.make_async_copy(tiles.at[axis, part], stage.at[axis, part], at)

    def bring(source, target, k):
        copy = pltpu.make_async_copy(source, target, sems.at[2 * chunks + k])
        copy.start()
        return copy

    small = [bring(x, y, k) for k, (x, y) in enumerate(((rows_in, rows), (block, v)))]
    for s in range(chunks):
        for axis in range(2):
            fetch(s, axis).start()
    nx, ny = lax.axis_size("gx"), lax.axis_size("gy")
    ix, iy = lax.axis_index("gx"), lax.axis_index("gy")
    for k, flag in enumerate((ix < nx - 1, ix > 0, iy < ny - 1, iy > 0, ix % 2 == 1, iy % 2 == 1)):
        flags[k] = flag.astype(jnp.int32)
    late = [bring(cols_in, cols, 3), bring(bounds_in, bounds, 4)]
    late.append(bring(stored.at[pl.ds(0, EARLY)], early, 5))
    for copy in small:
        copy.wait()
    v2[...] = stacked(v[...])
    shrunk(v, v8, jnp.max(jnp.abs(v[...]), axis=0), undo)

    def step(s, carry):
        outs = []
        for axis in range(2):
            fetch(s, axis).wait()
            for r in range(CHUNK):
                j = s * CHUNK + r
                high, low = split(stage[axis, j])
                ch[axis, j] = high
                cl[axis, j] = low
                dh[axis, j] = high.T
                dl[axis, j] = low.T
                outs.append((axis, j, two_piece(dot_nn, v2[rows[2 * axis, j]], high, low)))
        for axis, j, out in outs:
            send(rows, flags, v, axis, j, out, (a, b, c, d))
        return carry

    lax.fori_loop(0, chunks, step, 0)
    for copy in late:
        copy.wait()


def send(rows, flags, v, axis, j, product, sends):
    minus = v[rows[2 * axis + 1, j]]
    odd = flags[4 + axis] > 0
    sends[2 * axis][j] = jnp.where(odd, minus, product)
    sends[2 * axis + 1][j] = jnp.where(odd, product, minus)


def local_rows(rows, cols, v2, v8, undo, highs, lows, wf, wb):
    down = undo[...]
    wide = cat([down] * 4, axis=1)
    outs = []
    for i, high, low in zip(rows, highs, lows):
        at = [cols[k, i] for k in range(4)]
        high = cat(high, axis=1)
        low = cat(low, axis=1)
        forward = fold(dot_nt(cat([v2[c] for c in at], axis=1), high))
        forward = forward + down * fold(dot_nt(cat([v8[c] for c in at], axis=1), low))
        backward = fold(dot_nn(v2[i], high)) + wide * fold(dot_nn(v8[i], low))
        outs.append((forward, backward))
    for i, (forward, backward) in zip(rows, outs):
        wf[i] = forward
        for k in range(4):
            at = cols[k, i]
            wb[at] = wb[at] + backward[:, k * 128 : (k + 1) * 128]


def first_kernel(cols, v2, v8, undo, early, tiles, wf, wb, th, tl, stage, sems):
    copies = stage.shape[0] // ROWS

    def fetch(c):
        part = pl.ds(c * ROWS, ROWS)
        return pltpu.make_async_copy(
            tiles.at[pl.ds(EARLY + c * ROWS, ROWS)], stage.at[part], sems.at[c]
        )

    for c in range(copies):
        fetch(c).start()
    wb[...] = jnp.zeros_like(wb)

    def work(source, start, c):
        rows, highs, lows = [], [], []
        for r in range(ROWS):
            i = start + c * ROWS + r
            pieces = []
            for k in range(4):
                t = source[c * ROWS + r, k]
                high = t.astype(BF16)
                pieces.append((high, low_tile(t, high)))
            for k in range(4):
                th[i, k] = pieces[k][0]
                tl[i, k] = pieces[k][1]
            rows.append(i)
            highs.append([p[0] for p in pieces])
            lows.append([p[1] for p in pieces])
        local_rows(rows, cols, v2, v8, undo, highs, lows, wf, wb)

    def step_early(c, carry):
        work(early, 0, c)
        return carry

    def step(c, carry):
        fetch(c).wait()
        work(stage, EARLY, c)
        return carry

    lax.fori_loop(0, EARLY // ROWS, step_early, 0)
    lax.fori_loop(0, copies, step, 0)


def local_kernel(cols, v2, v8, undo, th, tl, wf, wb):
    wb[...] = jnp.zeros_like(wb)

    def step(c, carry):
        rows = [c * WIDE + r for r in range(WIDE)]
        highs = [[th[i, k] for k in range(4)] for i in rows]
        lows = [[tl[i, k] for k in range(4)] for i in rows]
        local_rows(rows, cols, v2, v8, undo, highs, lows, wf, wb)
        return carry

    lax.fori_loop(0, v2.shape[0] // WIDE, step, 0)


def arrive(rows, flags, received, dh, dl, acc):
    faces = rows.shape[1]

    def step(s, carry):
        outs = []
        for axis in range(2):
            odd = flags[4 + axis] > 0
            for r in range(FACES):
                j = s * FACES + r
                even, other = received[2 * axis][j], received[2 * axis + 1][j]
                u2 = stacked(jnp.where(flags[2 * axis] > 0, jnp.where(odd, other, even), 0.0))
                gain = two_piece(dot_nn, u2, dh[axis, j], dl[axis, j])
                outs.append((axis, j, gain, jnp.where(flags[2 * axis + 1] > 0, jnp.where(odd, even, other), 0.0)))
        for axis, j, gain, low in outs:
            place_rows(acc, rows, 2 * axis, gain, j)
            place_rows(acc, rows, 2 * axis + 1, low, j)
        return carry

    lax.fori_loop(0, faces // FACES, step, 0)


def next_kernel(order, rows, flags, bounds, *refs):
    if order == 1:
        (v, wf, wb, diag, ux, lx, uy, ly, dh, dl, ch, cl, *outs, acc) = refs
        older = None
    else:
        (v, older, wf, wb, diag, ux, lx, uy, ly, dh, dl, ch, cl, *outs, acc) = refs
    if order < 3:
        new, new2, new8, undo, *sends = outs
    else:
        new, new2, *sends = outs
    acc[...] = jnp.zeros_like(acc)
    arrive(rows, flags, (ux, lx, uy, ly), dh, dl, acc)
    lower = jnp.full((16, 128), bounds[0], F32)
    upper = jnp.full((16, 128), bounds[1], F32)
    half = (upper - lower) / 2.0
    centre = (upper + lower) / 2.0
    scale = (1.0 if order == 1 else 2.0) / half
    group = 8

    def step(s, carry):
        part = pl.ds(s * group, group)
        x = v[part]
        ax = wf[part] + wb[part] + acc[part] + diag[part][:, None, :] * x
        y = (ax - centre * x) * scale
        if older is not None:
            y = y - older[part]
        new[part] = y
        new2[part] = stacked(y)
        return jnp.maximum(carry, jnp.max(jnp.abs(y), axis=0))

    peak = lax.fori_loop(0, v.shape[0] // group, step, jnp.zeros((16, 128), F32))
    if order < 3:
        shrunk(new, new8, peak, undo)
        leave(new, new2, rows, flags, ch, cl, sends)
        return
    mx, my = sends

    def copy(j, carry):
        mx[j] = new[rows[1, j]]
        my[j] = new[rows[3, j]]
        return carry

    lax.fori_loop(0, rows.shape[1], copy, 0, unroll=8)


def quarter(total):
    half = total.shape[0] // 2
    return (total[:half, :half] + total[half:, half:]) + (total[:half, half:] + total[half:, :half])


def spread(out, gram, half):
    n = gram.shape[0]
    value = cat([cat([x[k : k + 2] for k in range(0, n, 2)], axis=1) for x in (gram, half)], axis=0)

    def step(d, carry):
        out[d] = value
        return carry

    lax.fori_loop(0, out.shape[0], step, 0)


def project_kernel(rows, cols, v, v2, diag, th, ch, out, over, gram, wb):
    group = 8

    def begin(s, carry):
        part = pl.ds(s * group, group)
        wb[part] = 0.5 * (diag[part][:, None, :] * v[part])
        return carry

    lax.fori_loop(0, v.shape[0] // group, begin, 0)

    def step(c, carry):
        outs = []
        for r in range(WIDE):
            i = c * WIDE + r
            outs.append((i, fold(dot_nn(v2[i], cat([th[i, k] for k in range(4)], axis=1)))))
        for i, backward in outs:
            for k in range(4):
                at = cols[k, i]
                wb[at] = wb[at] + backward[:, k * 128 : (k + 1) * 128]
        return carry

    lax.fori_loop(0, v.shape[0] // WIDE, step, 0)

    def face(s, carry):
        for axis in range(2):
            for r in range(CHUNK):
                j = s * CHUNK + r
                out = fold(dot_nn(v2[rows[2 * axis, j]], ch[axis, j]))
                over[axis, j] = stacked(out * SHRINK)
        return carry

    lax.fori_loop(0, rows.shape[1] // CHUNK, face, 0, unroll=True)
    total = other = jnp.zeros((32, 32), F32)
    for s in range(0, v.shape[0], 16):
        a2 = cat([v2[s + r] for r in range(16)], axis=1)
        b2 = cat([stacked(wb[s + r] * SHRINK) for r in range(16)], axis=1)
        total = total + dot_nt(a2, b2)
        other = other + dot_nt(a2, a2)
    out[...] = quarter(total)
    gram[...] = quarter(other)


def project_faces_kernel(flags, over, ux, uy, part, gram, out):
    total = jnp.zeros((32, 32), F32)
    for axis, upper in ((0, ux), (1, uy)):
        for s in range(0, upper.shape[0], CHUNK):
            lefts, rights = [], []
            for r in range(CHUNK):
                j = s + r
                rights.append(stacked(jnp.where(flags[2 * axis] > 0, upper[j], 0.0)))
                lefts.append(over[axis, j])
            total = total + dot_nt(cat(lefts, axis=1), cat(rights, axis=1))
    spread(out, gram[...], part[...] + quarter(total))


def end_kernel(nodes, sums, v2, out, projected, basis, sems):
    total = sums[0]
    for d in range(1, sums.shape[0]):
        total = total + sums[d]
    n = v2.shape[1] // 2
    g, half = (
        cat([total[k : k + 2, j : j + n] for j in range(0, n * n // 2, n)], axis=0) for k in (0, 2)
    )
    g = g / nodes
    row = lax.broadcasted_iota(jnp.int32, (n, n), 0)
    col = lax.broadcasted_iota(jnp.int32, (n, n), 1)
    m = cat([g, jnp.where(row == col, 1.0, 0.0).astype(F32)], axis=1)
    row = lax.broadcasted_iota(jnp.int32, m.shape, 0)
    pivots = jnp.zeros(m.shape, F32)
    for k in range(n):
        column = jnp.broadcast_to(m[:, k : k + 1], m.shape)
        pivots = jnp.where(row == k, column, pivots)
        factor = jnp.where(row > k, column * (1.0 / column[k : k + 1]), 0.0)
        m = m - factor * m[k : k + 1]
    inv = m[:, n:] / jnp.sqrt(pivots[:, n:])
    high, low = split(inv)
    left = cat([cat([high, high], axis=1), cat([low, jnp.zeros_like(low)], axis=1)], axis=0)
    group = 16
    copies = []
    for s in range(0, v2.shape[0], group):
        part = fold(dot_nn(left, cat([v2[s + r] for r in range(group)], axis=1)))
        for r in range(group):
            basis[s + r] = part[:, r * 128 : (r + 1) * 128]
        at = pl.ds(s, group)
        copies.append(pltpu.make_async_copy(basis.at[at], out.at[at], sems.at[s // group]))
        copies[-1].start()
    exact = dict(precision=lax.Precision.HIGHEST, preferred_element_type=F32)
    raw = lax.dot_general(inv, half, (((1,), (0,)), ((), ())), **exact)
    raw = lax.dot_general(raw, inv, (((1,), (1,)), ((), ())), **exact)
    projected[...] = (raw + raw.T) * (1.0 / (SHRINK * nodes))
    for copy in copies:
        copy.wait()


def in_hbm(x):
    return pltpu.with_memory_space_constraint(x, pltpu.HBM)


def in_vmem(shape, dtype):
    return pltpu.VMEM(shape, dtype)


def call(kernel, name, specs, outs, scratch=(), limit=12, flops=0, nbytes=0, smem=0, out_specs=None):
    return pl.pallas_call(
        kernel,
        name=name,
        in_specs=specs,
        out_specs=out_specs or [SM] * smem + [VM] * (len(outs) - smem),
        out_shape=outs,
        scratch_shapes=list(scratch),
        cost_estimate=pl.CostEstimate(flops=flops, bytes_accessed=nbytes, transcendentals=0),
        compiler_params=pltpu.CompilerParams(vmem_limit_bytes=limit * MIB),
    )


def ring(x, axis, by):
    peers = lax.axis_size(axis)
    return lax.ppermute(x, axis, [(i, (i + by) % peers) for i in range(peers)])


def pairs(x, axis, odd):
    nx, ny = lax.axis_size("gx"), lax.axis_size("gy")
    moves = []
    for u in range(nx):
        for w in range(ny):
            at, size = (u, nx) if axis == 0 else (w, ny)
            if odd and at in (0, size - 1):
                to = (u, w ^ 1) if axis == 0 else (u ^ 1, w)
            else:
                other = at + 1 if at % 2 == odd else at - 1
                to = (other, w) if axis == 0 else (u, other)
            moves.append((u * ny + w, to[0] * ny + to[1]))
    return lax.ppermute(x, ("gx", "gy"), moves)


def shards(start_block, tiles, tile_cols, node_diag, face_tiles, face_rows, filter_bounds):
    block = start_block[0, 0]
    stored = tiles[0, 0]
    cols = tile_cols[0, 0].T
    diag = node_diag[0, 0]
    coupling = face_tiles[0, 0]
    rows = face_rows[0, 0]
    count, width, tile = block.shape
    faces = rows.shape[1]
    nx, ny = lax.axis_size("gx"), lax.axis_size("gy")
    peers = nx * ny
    nodes = float(count * tile * peers)
    vec = in_vmem((count, width, tile), F32)
    vec2 = in_vmem((count, 2 * width, tile), BF16)
    vec8 = in_vmem((count, 2 * width, tile), F8)
    scale = in_vmem((width, tile), F32)
    face = jax.ShapeDtypeStruct((faces, width, tile), F32)
    high, low = in_vmem(stored.shape, BF16), in_vmem(stored.shape, F8)
    face2 = in_vmem(coupling.shape, BF16)
    square = in_vmem((width, width), F32)
    small = jax.ShapeDtypeStruct((peers, 4, 128), F32)
    local_flops = 16 * stored.size * width

    rows, cols, filter_bounds, flags, ch, cl, dh, dl, block, x2, x8, undo, *sends, early = call(
        begin_kernel, "begin", [HBM] * 6,
        [
            pltpu.SMEM(rows.shape, jnp.int32), pltpu.SMEM(cols.shape, jnp.int32),
            pltpu.SMEM((2,), F32), pltpu.SMEM((6,), jnp.int32),
            face2, face2, face2, face2, vec, vec2, vec8, scale, face, face, face, face,
            in_vmem((EARLY,) + stored.shape[1:], F32),
        ],
        [pltpu.VMEM(coupling.shape, F32), pltpu.SemaphoreType.DMA((2 * (faces // CHUNK) + 6,))],
        limit=8, flops=local_flops // 2, nbytes=4 * stored.size // 2, smem=4,
    )(*(in_hbm(x) for x in (rows, cols, filter_bounds, block, coupling, stored)))

    def exchange(sends):
        return tuple(pairs(x, k // 2, k % 2) for k, x in enumerate(sends))

    received = exchange(sends)
    wf, wb, th, tl = call(
        first_kernel, "local_first", [SM] + [VM] * 4 + [HBM], [vec, vec, high, low],
        [
            pltpu.VMEM((count - EARLY,) + stored.shape[1:], F32),
            pltpu.SemaphoreType.DMA(((count - EARLY) // ROWS,)),
        ],
        limit=24, flops=local_flops, nbytes=4 * stored.size,
    )(cols, x2, x8, undo, early, in_hbm(stored))

    x, older = block, None
    for order in (1, 2, 3):
        carried = (x,) if older is None else (x, older)
        last = order == 3
        outs = [vec, vec2] + ([face, face] if last else [vec8, scale] + [face] * 4)
        new, new2, *sends = call(
            functools.partial(next_kernel, order), "finish%d" % order,
            [SM, SM, SM] + [VM] * (11 + len(carried)), outs,
            [pltpu.VMEM((count, width, tile), F32)],
        )(rows, flags, filter_bounds, *carried, wf, wb, diag, *received, dh, dl, ch, cl)
        x, x2, older = new, new2, x
        if not last:
            x8, undo, *sends = sends
            received = exchange(sends)
            wf, wb = call(
                local_kernel, "local%d" % (order + 1), [SM] + [VM] * 5, [vec, vec],
                flops=local_flops, nbytes=4 * stored.size,
            )(cols, x2, x8, undo, th, tl)
    mx, my = sends
    ux, uy = ring(mx, "gx", -1), ring(my, "gy", -1)
    part, over, gram = call(
        project_kernel, "project", [SM, SM] + [VM] * 5,
        [square, in_vmem((2, faces, 2 * width, tile), BF16), square],
        [pltpu.VMEM((count, width, tile), F32)],
        flops=local_flops // 4, nbytes=2 * stored.size,
    )(rows, cols, x, x2, diag, th, ch)
    (sums,) = call(project_faces_kernel, "project_faces", [SM] + [VM] * 5, [small])(
        flags, over, ux, uy, part, gram
    )
    sums = lax.all_to_all(sums, ("gx", "gy"), 0, 0)
    basis, projected = call(
        functools.partial(end_kernel, nodes), "end", [VM, VM],
        [jax.ShapeDtypeStruct((count, width, tile), F32), jax.ShapeDtypeStruct((width, width), F32)],
        [pltpu.VMEM((count, width, tile), F32), pltpu.SemaphoreType.DMA((count // 16,))],
        out_specs=[HBM, VM],
    )(sums, x2)
    return (basis[None, None], projected)


def solution(mesh):
    in_specs = (
        P("gx", "gy", None, None, None),
        P("gx", "gy", None, None, None, None),
        P("gx", "gy", None, None),
        P("gx", "gy", None, None),
        P("gx", "gy", None, None, None, None),
        P("gx", "gy", None, None),
        P(),
    )
    out_specs = (P("gx", "gy", None, None, None), P())
    return jax.shard_map(shards, mesh=mesh, in_specs=in_specs, out_specs=out_specs, check_vma=False)
```

```python
import functools

import jax
import jax.numpy as jnp
from jax import lax
from jax.experimental import pallas as pl
from jax.experimental.pallas import tpu as pltpu
from jax.sharding import PartitionSpec as P

F32 = jnp.float32
BF16 = jnp.bfloat16
F8 = jnp.float8_e4m3fn
MIB = 1 << 20
VM = pl.BlockSpec(memory_space=pltpu.VMEM)
SM = pl.BlockSpec(memory_space=pltpu.SMEM)
HBM = pl.BlockSpec(memory_space=pltpu.HBM)
cat = jnp.concatenate

ROWS = 8
FACES = 24
WIDE = 32
CHUNK = 8
EARLY = 16
TILE_SCALE = 2.0**19
VEC_SCALE = 256.0
SHRINK = 1.0 / 64.0


def split(x):
    high = x.astype(BF16)
    low = (x - high.astype(F32)).astype(BF16)
    return high, low


def low_tile(t, high):
    return ((t - high.astype(F32)) * TILE_SCALE).astype(F8)


def stacked8(x):
    high = x.astype(F8)
    low = (x - high.astype(F32)).astype(F8)
    return cat([high, low], axis=-2)


def vector_scales(peak):
    top = jnp.maximum(jnp.max(peak, axis=1, keepdims=True), 1e-30)
    top = jnp.broadcast_to(top, peak.shape)
    return VEC_SCALE / top, top * (1.0 / (VEC_SCALE * TILE_SCALE))


def shrunk(v, v8, peak, undo):
    up, down = vector_scales(peak)
    undo[...] = down
    group = 8

    def step(s, carry):
        part = pl.ds(s * group, group)
        v8[part] = stacked8(v[part] * up)
        return carry

    lax.fori_loop(0, v.shape[0] // group, step, 0)


def stacked(x):
    return cat(split(x), axis=-2)


def dot_nn(x, t):
    return lax.dot_general(x, t, (((1,), (0,)), ((), ())), preferred_element_type=F32)


def dot_nt(x, t):
    return lax.dot_general(x, t, (((1,), (1,)), ((), ())), preferred_element_type=F32)


def fold(both, low=None):
    half = both.shape[0] // 2
    out = both[:half] + both[half:]
    return out if low is None else out + low


def two_piece(dot, x2, high, low):
    half = x2.shape[0] // 2
    return fold(dot(x2, high), dot(x2[:half], low))


def place_rows(w_ref, rows, which, data, j):
    at = rows[which, j]
    w_ref[at] = w_ref[at] + data


def leave(v, v2, rows, flags, ch, cl, sends):
    def step(s, carry):
        outs = []
        for axis in range(2):
            for r in range(FACES):
                j = s * FACES + r
                x2 = v2[rows[2 * axis, j]]
                outs.append((axis, j, two_piece(dot_nn, x2, ch[axis, j], cl[axis, j])))
        for axis, j, out in outs:
            send(rows, flags, v, axis, j, out, sends)
        return carry

    lax.fori_loop(0, rows.shape[1] // FACES, step, 0)


def begin_kernel(rows_in, cols_in, bounds_in, block, tiles, stored, *refs):
    (rows, cols, bounds, flags, ch, cl, dh, dl, v, v2, v8, undo, a, b, c, d, early, stage, sems) = refs
    faces = rows.shape[1]
    chunks = faces // CHUNK

    def fetch(s, axis):
        part = pl.ds(s * CHUNK, CHUNK)
        at = sems.at[2 * s + axis]
        return pltpu.make_async_copy(tiles.at[axis, part], stage.at[axis, part], at)

    def bring(source, target, k):
        copy = pltpu.make_async_copy(source, target, sems.at[2 * chunks + k])
        copy.start()
        return copy

    small = [bring(x, y, k) for k, (x, y) in enumerate(((rows_in, rows), (block, v)))]
    for s in range(chunks):
        for axis in range(2):
            fetch(s, axis).start()
    nx, ny = lax.axis_size("gx"), lax.axis_size("gy")
    ix, iy = lax.axis_index("gx"), lax.axis_index("gy")
    for k, flag in enumerate((ix < nx - 1, ix > 0, iy < ny - 1, iy > 0, ix % 2 == 1, iy % 2 == 1)):
        flags[k] = flag.astype(jnp.int32)
    late = [bring(cols_in, cols, 3), bring(bounds_in, bounds, 4)]
    late.append(bring(stored.at[pl.ds(0, EARLY)], early, 5))
    for copy in small:
        copy.wait()
    v2[...] = stacked(v[...])
    shrunk(v, v8, jnp.max(jnp.abs(v[...]), axis=0), undo)

    def step(s, carry):
        outs = []
        for axis in range(2):
            fetch(s, axis).wait()
            for r in range(CHUNK):
                j = s * CHUNK + r
                high, low = split(stage[axis, j])
                ch[axis, j] = high
                cl[axis, j] = low
                dh[axis, j] = high.T
                dl[axis, j] = low.T
                outs.append((axis, j, two_piece(dot_nn, v2[rows[2 * axis, j]], high, low)))
        for axis, j, out in outs:
            send(rows, flags, v, axis, j, out, (a, b, c, d))
        return carry

    lax.fori_loop(0, chunks, step, 0)
    for copy in late:
        copy.wait()


def send(rows, flags, v, axis, j, product, sends):
    minus = v[rows[2 * axis + 1, j]]
    odd = flags[4 + axis] > 0
    sends[2 * axis][j] = jnp.where(odd, minus, product)
    sends[2 * axis + 1][j] = jnp.where(odd, product, minus)


def local_rows(rows, cols, v2, v8, undo, pieces, wf, wb):
    down = undo[...]
    wide = cat([down] * 4, axis=1)
    outs = []
    for r, i in enumerate(rows):
        high, low, high_t, low_t = pieces(r, i)
        at = [cols[k, i] for k in range(4)]
        high = cat(high, axis=1)
        low = cat(low, axis=1)
        forward = fold(dot_nn(cat([v2[c] for c in at], axis=1), cat(high_t, axis=0)))
        forward = forward + down * fold(dot_nn(cat([v8[c] for c in at], axis=1), cat(low_t, axis=0)))
        backward = fold(dot_nn(v2[i], high)) + wide * fold(dot_nn(v8[i], low))
        outs.append((forward, backward))
    for i, (forward, backward) in zip(rows, outs):
        wf[i] = forward
        for k in range(4):
            at = cols[k, i]
            wb[at] = wb[at] + backward[:, k * 128 : (k + 1) * 128]


def first_kernel(cols, v2, v8, undo, early, tiles, wf, wb, th, tl, thT, tlT, stage, sems):
    copies = tiles.shape[0] // ROWS - EARLY // ROWS
    slots = stage.shape[0]
    ahead = slots - 1

    def fetch(c):
        slot = lax.rem(c, slots)
        part = pl.ds(EARLY + c * ROWS, ROWS)
        return pltpu.make_async_copy(tiles.at[part], stage.at[slot], sems.at[slot])

    for c in range(ahead):
        fetch(jnp.int32(c)).start()
    wb[...] = jnp.zeros_like(wb)

    def work(source, start):
        def pieces(r, i):
            made = [[], [], [], []]
            for k in range(4):
                t = source[r, k]
                high = t.astype(BF16)
                low = low_tile(t, high)
                for out, ref, x in zip(made, (th, tl, thT, tlT), (high, low, high.T, low.T)):
                    ref[i, k] = x
                    out.append(x)
            return made

        local_rows([start + r for r in range(ROWS)], cols, v2, v8, undo, pieces, wf, wb)

    def step_early(c, carry):
        work(early.at[pl.ds(c * ROWS, ROWS)], c * ROWS)
        return carry

    def step(c, carry):
        fetch(c).wait()

        @pl.when(c + ahead < copies)
        def _():
            fetch(c + ahead).start()

        work(stage.at[lax.rem(c, slots)], EARLY + c * ROWS)
        return carry

    lax.fori_loop(0, EARLY // ROWS, step_early, 0)
    lax.fori_loop(0, copies, step, 0)


def local_kernel(cols, v2, v8, undo, th, tl, thT, tlT, wf, wb):
    wb[...] = jnp.zeros_like(wb)

    def step(c, carry):
        rows = [c * WIDE + r for r in range(WIDE)]

        def pieces(r, i):
            return [[ref[i, k] for k in range(4)] for ref in (th, tl, thT, tlT)]

        local_rows(rows, cols, v2, v8, undo, pieces, wf, wb)
        return carry

    lax.fori_loop(0, v2.shape[0] // WIDE, step, 0)


def arrive(rows, flags, received, dh, dl, acc):
    faces = rows.shape[1]

    def step(s, carry):
        outs = []
        for axis in range(2):
            odd = flags[4 + axis] > 0
            for r in range(FACES):
                j = s * FACES + r
                even, other = received[2 * axis][j], received[2 * axis + 1][j]
                u2 = stacked(jnp.where(flags[2 * axis] > 0, jnp.where(odd, other, even), 0.0))
                gain = two_piece(dot_nn, u2, dh[axis, j], dl[axis, j])
                outs.append((axis, j, gain, jnp.where(flags[2 * axis + 1] > 0, jnp.where(odd, even, other), 0.0)))
        for axis, j, gain, low in outs:
            place_rows(acc, rows, 2 * axis, gain, j)
            place_rows(acc, rows, 2 * axis + 1, low, j)
        return carry

    lax.fori_loop(0, faces // FACES, step, 0)


def next_kernel(order, rows, flags, bounds, *refs):
    if order == 1:
        (v, wf, wb, diag, ux, lx, uy, ly, dh, dl, ch, cl, *outs, acc) = refs
        older = None
    else:
        (v, older, wf, wb, diag, ux, lx, uy, ly, dh, dl, ch, cl, *outs, acc) = refs
    if order < 3:
        new, new2, new8, undo, *sends = outs
    else:
        new, new2, *sends = outs
    acc[...] = jnp.zeros_like(acc)
    arrive(rows, flags, (ux, lx, uy, ly), dh, dl, acc)
    lower = jnp.full((16, 128), bounds[0], F32)
    upper = jnp.full((16, 128), bounds[1], F32)
    half = (upper - lower) / 2.0
    centre = (upper + lower) / 2.0
    scale = (1.0 if order == 1 else 2.0) / half
    group = 8

    def step(s, carry):
        part = pl.ds(s * group, group)
        x = v[part]
        ax = wf[part] + wb[part] + acc[part] + diag[part][:, None, :] * x
        y = (ax - centre * x) * scale
        if older is not None:
            y = y - older[part]
        new[part] = y
        new2[part] = stacked(y)
        return jnp.maximum(carry, jnp.max(jnp.abs(y), axis=0))

    peak = lax.fori_loop(0, v.shape[0] // group, step, jnp.zeros((16, 128), F32))
    if order < 3:
        shrunk(new, new8, peak, undo)
        leave(new, new2, rows, flags, ch, cl, sends)
        return
    last_sends(new, new2, rows, flags, ch, sends)


def last_sends(v, v2, rows, flags, ch, sends):
    part = rows.shape[1] // 2
    outs = []
    for axis in range(2):
        for j in range(part):
            outs.append((axis, j, fold(dot_nn(v2[rows[2 * axis, j]], ch[axis, j]))))
    for axis, j, out in outs:
        minus = v[rows[2 * axis + 1, part + j]]
        odd = flags[4 + axis] > 0
        sends[2 * axis][j] = jnp.where(odd, minus, out)
        sends[2 * axis + 1][j] = jnp.where(odd, out, minus)


def quarter(total):
    half = total.shape[0] // 2
    return (total[:half, :half] + total[half:, half:]) + (total[:half, half:] + total[half:, :half])


def spread(out, gram, half):
    n = gram.shape[0]
    value = cat([cat([x[k : k + 2] for k in range(0, n, 2)], axis=1) for x in (gram, half)], axis=0)

    def step(d, carry):
        out[d] = value
        return carry

    lax.fori_loop(0, out.shape[0], step, 0)


def project_kernel(rows, cols, v, v2, diag, th, ch, out, over, gram, wb):
    group = 8

    def begin(s, carry):
        part = pl.ds(s * group, group)
        wb[part] = 0.5 * (diag[part][:, None, :] * v[part])
        return carry

    lax.fori_loop(0, v.shape[0] // group, begin, 0)

    def step(c, carry):
        outs = []
        for r in range(WIDE):
            i = c * WIDE + r
            outs.append((i, fold(dot_nn(v2[i], cat([th[i, k] for k in range(4)], axis=1)))))
        for i, backward in outs:
            for k in range(4):
                at = cols[k, i]
                wb[at] = wb[at] + backward[:, k * 128 : (k + 1) * 128]
        return carry

    lax.fori_loop(0, v.shape[0] // WIDE, step, 0)

    part = over.shape[1]
    for axis in range(2):
        for j in range(part):
            product = fold(dot_nn(v2[rows[2 * axis, part + j]], ch[axis, part + j]))
            over[axis, j] = stacked(product * SHRINK)
    total = other = jnp.zeros((32, 32), F32)
    for s in range(0, v.shape[0], 16):
        a2 = cat([v2[s + r] for r in range(16)], axis=1)
        b2 = cat([stacked(wb[s + r] * SHRINK) for r in range(16)], axis=1)
        total = total + dot_nt(a2, b2)
        other = other + dot_nt(a2, a2)
    out[...] = quarter(total)
    gram[...] = quarter(other)


def project_faces_kernel(rows, flags, v2, over, xe, xo, ye, yo, part, gram, out):
    total = jnp.zeros((32, 32), F32)
    count = xe.shape[0]
    for axis, (even, odd) in enumerate(((xe, xo), (ye, yo))):
        swapped = flags[4 + axis] > 0
        lefts, rights = [], []
        for j in range(count):
            e, o = even[j], odd[j]
            above = jnp.where(flags[2 * axis] > 0, jnp.where(swapped, o, e), 0.0)
            below = jnp.where(flags[2 * axis + 1] > 0, jnp.where(swapped, e, o), 0.0)
            lefts += [over[axis, j], stacked(below * SHRINK)]
            rights += [stacked(above), v2[rows[2 * axis + 1, j]]]
        total = total + dot_nt(cat(lefts, axis=1), cat(rights, axis=1))
    spread(out, gram[...], part[...] + quarter(total))


def end_kernel(nodes, sums, v2, out, projected, basis, sems):
    total = sums[0]
    for d in range(1, sums.shape[0]):
        total = total + sums[d]
    n = v2.shape[1] // 2
    g, half = (
        cat([total[k : k + 2, j : j + n] for j in range(0, n * n // 2, n)], axis=0) for k in (0, 2)
    )
    g = g / nodes
    row = lax.broadcasted_iota(jnp.int32, (n, n), 0)
    col = lax.broadcasted_iota(jnp.int32, (n, n), 1)
    m = cat([g, jnp.where(row == col, 1.0, 0.0).astype(F32)], axis=1)
    row = lax.broadcasted_iota(jnp.int32, m.shape, 0)
    pivots = jnp.zeros(m.shape, F32)
    for k in range(0, n, 2):
        first = jnp.broadcast_to(m[:, k : k + 1], m.shape)
        second = jnp.broadcast_to(m[:, k + 1 : k + 2], m.shape)
        pivots = jnp.where(row == k, first, pivots)
        ratio = 1.0 / first[k : k + 1]
        step = first[k + 1 : k + 2] * ratio
        second = second - first * (second[k : k + 1] * ratio)
        pivots = jnp.where(row == k + 1, second, pivots)
        top = m[k : k + 1]
        below = m[k + 1 : k + 2] - step * top
        factor = jnp.where(row > k, first * ratio, 0.0)
        other = jnp.where(row > k + 1, second * (1.0 / second[k + 1 : k + 2]), 0.0)
        m = m - factor * top - other * below
    inv = m[:, n:] / jnp.sqrt(pivots[:, n:])
    high, low = split(inv)
    left = cat([cat([high, high], axis=1), cat([low, jnp.zeros_like(low)], axis=1)], axis=0)
    group = 16
    copies = []
    for s in range(0, v2.shape[0], group):
        part = fold(dot_nn(left, cat([v2[s + r] for r in range(group)], axis=1)))
        for r in range(group):
            basis[s + r] = part[:, r * 128 : (r + 1) * 128]
        at = pl.ds(s, group)
        copies.append(pltpu.make_async_copy(basis.at[at], out.at[at], sems.at[s // group]))
        copies[-1].start()
    exact = dict(precision=lax.Precision.HIGHEST, preferred_element_type=F32)
    raw = lax.dot_general(inv, half, (((1,), (0,)), ((), ())), **exact)
    raw = lax.dot_general(raw, inv, (((1,), (1,)), ((), ())), **exact)
    projected[...] = (raw + raw.T) * (1.0 / (SHRINK * nodes))
    for copy in copies:
        copy.wait()


def in_hbm(x):
    return pltpu.with_memory_space_constraint(x, pltpu.HBM)


def in_vmem(shape, dtype):
    return pltpu.VMEM(shape, dtype)


def call(kernel, name, specs, outs, scratch=(), limit=12, flops=0, nbytes=0, smem=0, out_specs=None):
    return pl.pallas_call(
        kernel,
        name=name,
        in_specs=specs,
        out_specs=out_specs or [SM] * smem + [VM] * (len(outs) - smem),
        out_shape=outs,
        scratch_shapes=list(scratch),
        cost_estimate=pl.CostEstimate(flops=flops, bytes_accessed=nbytes, transcendentals=0),
        compiler_params=pltpu.CompilerParams(vmem_limit_bytes=limit * MIB),
    )


def pairs(x, axis, odd):
    nx, ny = lax.axis_size("gx"), lax.axis_size("gy")
    moves = []
    for u in range(nx):
        for w in range(ny):
            at, size = (u, nx) if axis == 0 else (w, ny)
            if odd and at in (0, size - 1):
                to = (u, w ^ 1) if axis == 0 else (u ^ 1, w)
            else:
                other = at + 1 if at % 2 == odd else at - 1
                to = (other, w) if axis == 0 else (u, other)
            moves.append((u * ny + w, to[0] * ny + to[1]))
    return lax.ppermute(x, ("gx", "gy"), moves)


def shards(start_block, tiles, tile_cols, node_diag, face_tiles, face_rows, filter_bounds):
    block = start_block[0, 0]
    stored = tiles[0, 0]
    cols = tile_cols[0, 0].T
    diag = node_diag[0, 0]
    coupling = face_tiles[0, 0]
    rows = face_rows[0, 0]
    count, width, tile = block.shape
    faces = rows.shape[1]
    nx, ny = lax.axis_size("gx"), lax.axis_size("gy")
    peers = nx * ny
    nodes = float(count * tile * peers)
    vec = in_vmem((count, width, tile), F32)
    vec2 = in_vmem((count, 2 * width, tile), BF16)
    vec8 = in_vmem((count, 2 * width, tile), F8)
    scale = in_vmem((width, tile), F32)
    half_face = jax.ShapeDtypeStruct((faces // 2, width, tile), F32)
    face = jax.ShapeDtypeStruct((faces, width, tile), F32)
    high, low = in_vmem(stored.shape, BF16), in_vmem(stored.shape, F8)
    face2 = in_vmem(coupling.shape, BF16)
    square = in_vmem((width, width), F32)
    small = jax.ShapeDtypeStruct((peers, 4, 128), F32)
    local_flops = 16 * stored.size * width

    rows, cols, filter_bounds, flags, ch, cl, dh, dl, block, x2, x8, undo, *sends, early = call(
        begin_kernel, "begin", [HBM] * 6,
        [
            pltpu.SMEM(rows.shape, jnp.int32), pltpu.SMEM(cols.shape, jnp.int32),
            pltpu.SMEM((2,), F32), pltpu.SMEM((6,), jnp.int32),
            face2, face2, face2, face2, vec, vec2, vec8, scale, face, face, face, face,
            in_vmem((EARLY,) + stored.shape[1:], F32),
        ],
        [pltpu.VMEM(coupling.shape, F32), pltpu.SemaphoreType.DMA((2 * (faces // CHUNK) + 6,))],
        limit=8, flops=local_flops // 2, nbytes=4 * stored.size // 2, smem=4,
    )(*(in_hbm(x) for x in (rows, cols, filter_bounds, block, coupling, stored)))

    def exchange(sends):
        return tuple(pairs(x, k // 2, k % 2) for k, x in enumerate(sends))

    received = exchange(sends)
    wf, wb, th, tl, thT, tlT = call(
        first_kernel, "local_first", [SM] + [VM] * 4 + [HBM], [vec, vec, high, low, high, low],
        [
            pltpu.VMEM((4, ROWS) + stored.shape[1:], F32),
            pltpu.SemaphoreType.DMA((4,)),
        ],
        limit=16, flops=local_flops, nbytes=4 * stored.size,
    )(cols, x2, x8, undo, early, in_hbm(stored))

    x, older = block, None
    for order in (1, 2, 3):
        carried = (x,) if older is None else (x, older)
        last = order == 3
        outs = [vec, vec2] + ([half_face] * 4 if last else [vec8, scale] + [face] * 4)
        new, new2, *sends = call(
            functools.partial(next_kernel, order), "finish%d" % order,
            [SM, SM, SM] + [VM] * (11 + len(carried)), outs,
            [pltpu.VMEM((count, width, tile), F32)],
        )(rows, flags, filter_bounds, *carried, wf, wb, diag, *received, dh, dl, ch, cl)
        x, x2, older = new, new2, x
        if not last:
            x8, undo, *sends = sends
            received = exchange(sends)
            wf, wb = call(
                local_kernel, "local%d" % (order + 1), [SM] + [VM] * 7, [vec, vec],
                flops=local_flops, nbytes=4 * stored.size,
            )(cols, x2, x8, undo, th, tl, thT, tlT)
    received = exchange(sends)
    part, over, gram = call(
        project_kernel, "project", [SM, SM] + [VM] * 5,
        [square, in_vmem((2, faces // 2, 2 * width, tile), BF16), square],
        [pltpu.VMEM((count, width, tile), F32)],
        flops=local_flops // 4, nbytes=2 * stored.size,
    )(rows, cols, x, x2, diag, th, ch)
    (sums,) = call(project_faces_kernel, "project_faces", [SM, SM] + [VM] * 8, [small])(
        rows, flags, x2, over, *received, part, gram
    )
    sums = lax.all_to_all(sums, ("gx", "gy"), 0, 0)
    basis, projected = call(
        functools.partial(end_kernel, nodes), "end", [VM, VM],
        [jax.ShapeDtypeStruct((count, width, tile), F32), jax.ShapeDtypeStruct((width, width), F32)],
        [pltpu.VMEM((count, width, tile), F32), pltpu.SemaphoreType.DMA((count // 16,))],
        out_specs=[HBM, VM],
    )(sums, x2)
    return (basis[None, None], projected)


def solution(mesh):
    in_specs = (
        P("gx", "gy", None, None, None),
        P("gx", "gy", None, None, None, None),
        P("gx", "gy", None, None),
        P("gx", "gy", None, None),
        P("gx", "gy", None, None, None, None),
        P("gx", "gy", None, None),
        P(),
    )
    out_specs = (P("gx", "gy", None, None, None), P())
    return jax.shard_map(shards, mesh=mesh, in_specs=in_specs, out_specs=out_specs, check_vma=False)
```

```python
import functools

import jax
import jax.numpy as jnp
from jax import lax
from jax.experimental import pallas as pl
from jax.experimental.pallas import tpu as pltpu
from jax.sharding import PartitionSpec as P

F32 = jnp.float32
BF16 = jnp.bfloat16
F8 = jnp.float8_e4m3fn
MIB = 1 << 20
VM = pl.BlockSpec(memory_space=pltpu.VMEM)
SM = pl.BlockSpec(memory_space=pltpu.SMEM)
HBM = pl.BlockSpec(memory_space=pltpu.HBM)
cat = jnp.concatenate

ROWS = 8
FACES = 24
WIDE = 64
CHUNK = 12
EARLY = 16
TILE_SCALE = 2.0**19
VEC_SCALE = 256.0
SHRINK = 1.0 / 64.0


def split(x):
    high = x.astype(BF16)
    low = (x - high.astype(F32)).astype(BF16)
    return high, low


def low_tile(t, high):
    return ((t - high.astype(F32)) * TILE_SCALE).astype(F8)


def stacked8(x):
    high = x.astype(F8)
    low = (x - high.astype(F32)).astype(F8)
    return cat([high, low], axis=-2)


def vector_scales(peak):
    top = jnp.maximum(jnp.max(peak, axis=1, keepdims=True), 1e-30)
    top = jnp.broadcast_to(top, peak.shape)
    return VEC_SCALE / top, top * (1.0 / (VEC_SCALE * TILE_SCALE))


def shrunk(v, v8, peak, undo):
    up, down = vector_scales(peak)
    undo[...] = down
    group = 16

    def step(s, carry):
        part = pl.ds(s * group, group)
        v8[part] = stacked8(v[part] * up)
        return carry

    lax.fori_loop(0, v.shape[0] // group, step, 0)


def stacked(x):
    return cat(split(x), axis=-2)


def dot_nn(x, t):
    return lax.dot_general(x, t, (((1,), (0,)), ((), ())), preferred_element_type=F32)


def dot_nt(x, t):
    return lax.dot_general(x, t, (((1,), (1,)), ((), ())), preferred_element_type=F32)


def fold(both, low=None):
    half = both.shape[0] // 2
    out = both[:half] + both[half:]
    return out if low is None else out + low


def two_piece(dot, x2, high, low):
    half = x2.shape[0] // 2
    return fold(dot(x2, high), dot(x2[:half], low))


def place_rows(w_ref, rows, which, data, j):
    at = rows[which, j]
    w_ref[at] = w_ref[at] + data


def leave(v, v2, rows, flags, ch, cl, sends):
    def step(s, carry):
        outs = []
        for axis in range(2):
            for r in range(FACES):
                j = s * FACES + r
                x2 = v2[rows[2 * axis, j]]
                outs.append((axis, j, two_piece(dot_nn, x2, ch[axis, j], cl[axis, j])))
        for axis, j, out in outs:
            send(rows, flags, v, axis, j, out, sends)
        return carry

    lax.fori_loop(0, rows.shape[1] // FACES, step, 0)


def begin_kernel(rows_in, cols_in, bounds_in, block, tiles, stored, *refs):
    (rows, cols, bounds, flags, ch, cl, dh, dl, v, v2, v8, undo, a, b, c, d, early, stage, sems) = refs
    faces = rows.shape[1]
    chunks = faces // CHUNK

    def fetch(s, axis):
        part = pl.ds(s * CHUNK, CHUNK)
        at = sems.at[2 * s + axis]
        return pltpu.make_async_copy(tiles.at[axis, part], stage.at[axis, part], at)

    def bring(source, target, k):
        copy = pltpu.make_async_copy(source, target, sems.at[2 * chunks + k])
        copy.start()
        return copy

    small = [bring(x, y, k) for k, (x, y) in enumerate(((rows_in, rows), (block, v)))]
    for s in range(chunks):
        for axis in range(2):
            fetch(s, axis).start()
    nx, ny = lax.axis_size("gx"), lax.axis_size("gy")
    ix, iy = lax.axis_index("gx"), lax.axis_index("gy")
    for k, flag in enumerate((ix < nx - 1, ix > 0, iy < ny - 1, iy > 0, ix % 2 == 1, iy % 2 == 1)):
        flags[k] = flag.astype(jnp.int32)
    late = [bring(cols_in, cols, 3), bring(bounds_in, bounds, 4)]
    late.append(bring(stored.at[pl.ds(0, EARLY)], early, 5))
    for copy in small:
        copy.wait()
    v2[...] = stacked(v[...])
    shrunk(v, v8, jnp.max(jnp.abs(v[...]), axis=0), undo)

    def step(s, carry):
        outs = []
        for axis in range(2):
            fetch(s, axis).wait()
            for r in range(CHUNK):
                j = s * CHUNK + r
                high, low = split(stage[axis, j])
                ch[axis, j] = high
                cl[axis, j] = low
                dh[axis, j] = high.T
                dl[axis, j] = low.T
                outs.append((axis, j, two_piece(dot_nn, v2[rows[2 * axis, j]], high, low)))
        for axis, j, out in outs:
            send(rows, flags, v, axis, j, out, (a, b, c, d))
        return carry

    lax.fori_loop(0, chunks, step, 0)
    for copy in late:
        copy.wait()


def send(rows, flags, v, axis, j, product, sends):
    minus = v[rows[2 * axis + 1, j]]
    odd = flags[4 + axis] > 0
    sends[2 * axis][j] = jnp.where(odd, minus, product)
    sends[2 * axis + 1][j] = jnp.where(odd, product, minus)


def local_rows(rows, cols, v2, v8, undo, pieces, wf, wb):
    down = undo[...]
    wide = cat([down] * 4, axis=1)
    outs = []
    for r, i in enumerate(rows):
        high, low, high_t, low_t = pieces(r, i)
        at = [cols[k, i] for k in range(4)]
        high = cat(high, axis=1)
        low = cat(low, axis=1)
        forward = fold(dot_nn(cat([v2[c] for c in at], axis=1), cat(high_t, axis=0)))
        forward = forward + down * fold(dot_nn(cat([v8[c] for c in at], axis=1), cat(low_t, axis=0)))
        backward = fold(dot_nn(v2[i], high)) + wide * fold(dot_nn(v8[i], low))
        outs.append((forward, backward))
    for i, (forward, backward) in zip(rows, outs):
        wf[i] = forward
        for k in range(4):
            at = cols[k, i]
            wb[at] = wb[at] + backward[:, k * 128 : (k + 1) * 128]


def first_kernel(cols, v2, v8, undo, early, tiles, wf, wb, th, tl, thT, tlT, stage, sems):
    copies = tiles.shape[0] // ROWS - EARLY // ROWS
    slots = stage.shape[0]
    ahead = slots - 1

    def fetch(c):
        slot = lax.rem(c, slots)
        part = pl.ds(EARLY + c * ROWS, ROWS)
        return pltpu.make_async_copy(tiles.at[part], stage.at[slot], sems.at[slot])

    for c in range(ahead):
        fetch(jnp.int32(c)).start()
    wb[...] = jnp.zeros_like(wb)

    def work(source, start):
        def pieces(r, i):
            made = [[], [], [], []]
            for k in range(4):
                t = source[r, k]
                high = t.astype(BF16)
                low = low_tile(t, high)
                for out, ref, x in zip(made, (th, tl, thT, tlT), (high, low, high.T, low.T)):
                    ref[i, k] = x
                    out.append(x)
            return made

        local_rows([start + r for r in range(ROWS)], cols, v2, v8, undo, pieces, wf, wb)

    def step_early(c, carry):
        work(early.at[pl.ds(c * ROWS, ROWS)], c * ROWS)
        return carry

    def step(c, carry):
        fetch(c).wait()

        @pl.when(c + ahead < copies)
        def _():
            fetch(c + ahead).start()

        work(stage.at[lax.rem(c, slots)], EARLY + c * ROWS)
        return carry

    lax.fori_loop(0, EARLY // ROWS, step_early, 0)
    lax.fori_loop(0, copies, step, 0)


def local_kernel(cols, v2, v8, undo, th, tl, thT, tlT, wf, wb):
    wb[...] = jnp.zeros_like(wb)

    def step(c, carry):
        rows = [c * WIDE + r for r in range(WIDE)]

        def pieces(r, i):
            return [[ref[i, k] for k in range(4)] for ref in (th, tl, thT, tlT)]

        local_rows(rows, cols, v2, v8, undo, pieces, wf, wb)
        return carry

    lax.fori_loop(0, v2.shape[0] // WIDE, step, 0)


def arrive(rows, flags, received, dh, dl, acc):
    faces = rows.shape[1]

    def step(s, carry):
        outs = []
        for axis in range(2):
            odd = flags[4 + axis] > 0
            for r in range(FACES):
                j = s * FACES + r
                even, other = received[2 * axis][j], received[2 * axis + 1][j]
                u2 = stacked(jnp.where(flags[2 * axis] > 0, jnp.where(odd, other, even), 0.0))
                gain = two_piece(dot_nn, u2, dh[axis, j], dl[axis, j])
                outs.append((axis, j, gain, jnp.where(flags[2 * axis + 1] > 0, jnp.where(odd, even, other), 0.0)))
        for axis, j, gain, low in outs:
            place_rows(acc, rows, 2 * axis, gain, j)
            place_rows(acc, rows, 2 * axis + 1, low, j)
        return carry

    lax.fori_loop(0, faces // FACES, step, 0)


def next_kernel(order, rows, flags, bounds, *refs):
    if order == 1:
        (v, wf, wb, diag, ux, lx, uy, ly, dh, dl, ch, cl, *outs, acc) = refs
        older = None
    else:
        (v, older, wf, wb, diag, ux, lx, uy, ly, dh, dl, ch, cl, *outs, acc) = refs
    if order < 3:
        new, new2, new8, undo, *sends = outs
    else:
        new, new2, *sends = outs
    acc[...] = jnp.zeros_like(acc)
    arrive(rows, flags, (ux, lx, uy, ly), dh, dl, acc)
    lower = jnp.full((16, 128), bounds[0], F32)
    upper = jnp.full((16, 128), bounds[1], F32)
    half = (upper - lower) / 2.0
    centre = (upper + lower) / 2.0
    scale = (1.0 if order == 1 else 2.0) / half
    group = 16

    def step(s, carry):
        part = pl.ds(s * group, group)
        x = v[part]
        ax = wf[part] + wb[part] + acc[part] + diag[part][:, None, :] * x
        y = (ax - centre * x) * scale
        if older is not None:
            y = y - older[part]
        new[part] = y
        new2[part] = stacked(y)
        return jnp.maximum(carry, jnp.max(jnp.abs(y), axis=0))

    peak = lax.fori_loop(0, v.shape[0] // group, step, jnp.zeros((16, 128), F32))
    if order < 3:
        shrunk(new, new8, peak, undo)
        leave(new, new2, rows, flags, ch, cl, sends)
        return
    last_sends(new, new2, rows, flags, ch, sends)


def last_sends(v, v2, rows, flags, ch, sends):
    part = rows.shape[1] // 2
    outs = []
    for axis in range(2):
        for j in range(part):
            outs.append((axis, j, fold(dot_nn(v2[rows[2 * axis, j]], ch[axis, j]))))
    for axis, j, out in outs:
        minus = v[rows[2 * axis + 1, part + j]]
        odd = flags[4 + axis] > 0
        sends[2 * axis][j] = jnp.where(odd, minus, out)
        sends[2 * axis + 1][j] = jnp.where(odd, out, minus)


def quarter(total):
    half = total.shape[0] // 2
    return (total[:half, :half] + total[half:, half:]) + (total[:half, half:] + total[half:, :half])


def spread(out, gram, half):
    n = gram.shape[0]
    value = cat([cat([x[k : k + 2] for k in range(0, n, 2)], axis=1) for x in (gram, half)], axis=0)

    def step(d, carry):
        out[d] = value
        return carry

    lax.fori_loop(0, out.shape[0], step, 0)


def project_kernel(rows, cols, v, v2, diag, th, ch, out, over, gram, wb):
    group = 8

    def begin(s, carry):
        part = pl.ds(s * group, group)
        wb[part] = 0.5 * (diag[part][:, None, :] * v[part])
        return carry

    lax.fori_loop(0, v.shape[0] // group, begin, 0)

    def step(c, carry):
        outs = []
        for r in range(WIDE):
            i = c * WIDE + r
            outs.append((i, fold(dot_nn(v2[i], cat([th[i, k] for k in range(4)], axis=1)))))
        for i, backward in outs:
            for k in range(4):
                at = cols[k, i]
                wb[at] = wb[at] + backward[:, k * 128 : (k + 1) * 128]
        return carry

    lax.fori_loop(0, v.shape[0] // WIDE, step, 0)

    part = over.shape[1]
    for axis in range(2):
        for j in range(part):
            product = fold(dot_nn(v2[rows[2 * axis, part + j]], ch[axis, part + j]))
            over[axis, j] = stacked(product * SHRINK)
    total = other = jnp.zeros((32, 32), F32)
    for s in range(0, v.shape[0], 16):
        a2 = cat([v2[s + r] for r in range(16)], axis=1)
        b2 = cat([stacked(wb[s + r] * SHRINK) for r in range(16)], axis=1)
        total = total + dot_nt(a2, b2)
        other = other + dot_nt(a2, a2)
    out[...] = quarter(total)
    gram[...] = quarter(other)


def project_faces_kernel(rows, flags, v2, over, xe, xo, ye, yo, part, gram, out):
    total = jnp.zeros((32, 32), F32)
    count = xe.shape[0]
    for axis, (even, odd) in enumerate(((xe, xo), (ye, yo))):
        swapped = flags[4 + axis] > 0
        lefts, rights = [], []
        for j in range(count):
            e, o = even[j], odd[j]
            above = jnp.where(flags[2 * axis] > 0, jnp.where(swapped, o, e), 0.0)
            below = jnp.where(flags[2 * axis + 1] > 0, jnp.where(swapped, e, o), 0.0)
            lefts += [over[axis, j], stacked(below * SHRINK)]
            rights += [stacked(above), v2[rows[2 * axis + 1, j]]]
        total = total + dot_nt(cat(lefts, axis=1), cat(rights, axis=1))
    spread(out, gram[...], part[...] + quarter(total))


def end_kernel(nodes, sums, v2, out, projected, basis, sems):
    total = sums[0]
    for d in range(1, sums.shape[0]):
        total = total + sums[d]
    n = v2.shape[1] // 2
    g, half = (
        cat([total[k : k + 2, j : j + n] for j in range(0, n * n // 2, n)], axis=0) for k in (0, 2)
    )
    g = g / nodes
    row = lax.broadcasted_iota(jnp.int32, (n, n), 0)
    col = lax.broadcasted_iota(jnp.int32, (n, n), 1)
    m = cat([g, jnp.where(row == col, 1.0, 0.0).astype(F32)], axis=1)
    row = lax.broadcasted_iota(jnp.int32, m.shape, 0)
    pivots = jnp.zeros(m.shape, F32)
    for k in range(0, n, 2):
        first = jnp.broadcast_to(m[:, k : k + 1], m.shape)
        second = jnp.broadcast_to(m[:, k + 1 : k + 2], m.shape)
        pivots = jnp.where(row == k, first, pivots)
        ratio = 1.0 / first[k : k + 1]
        step = first[k + 1 : k + 2] * ratio
        second = second - first * (second[k : k + 1] * ratio)
        pivots = jnp.where(row == k + 1, second, pivots)
        top = m[k : k + 1]
        below = m[k + 1 : k + 2] - step * top
        factor = jnp.where(row > k, first * ratio, 0.0)
        other = jnp.where(row > k + 1, second * (1.0 / second[k + 1 : k + 2]), 0.0)
        m = m - factor * top - other * below
    inv = m[:, n:] / jnp.sqrt(pivots[:, n:])
    high, low = split(inv)
    left = cat([cat([high, high], axis=1), cat([low, jnp.zeros_like(low)], axis=1)], axis=0)
    group = 16
    copies = []
    for s in range(0, v2.shape[0], group):
        part = fold(dot_nn(left, cat([v2[s + r] for r in range(group)], axis=1)))
        for r in range(group):
            basis[s + r] = part[:, r * 128 : (r + 1) * 128]
        at = pl.ds(s, group)
        copies.append(pltpu.make_async_copy(basis.at[at], out.at[at], sems.at[s // group]))
        copies[-1].start()
    exact = dict(precision=lax.Precision.HIGHEST, preferred_element_type=F32)
    raw = lax.dot_general(inv, half, (((1,), (0,)), ((), ())), **exact)
    raw = lax.dot_general(raw, inv, (((1,), (1,)), ((), ())), **exact)
    projected[...] = (raw + raw.T) * (1.0 / (SHRINK * nodes))
    for copy in copies:
        copy.wait()


def in_hbm(x):
    return pltpu.with_memory_space_constraint(x, pltpu.HBM)


def in_vmem(shape, dtype):
    return pltpu.VMEM(shape, dtype)


def call(kernel, name, specs, outs, scratch=(), limit=12, flops=0, nbytes=0, smem=0, out_specs=None):
    return pl.pallas_call(
        kernel,
        name=name,
        in_specs=specs,
        out_specs=out_specs or [SM] * smem + [VM] * (len(outs) - smem),
        out_shape=outs,
        scratch_shapes=list(scratch),
        cost_estimate=pl.CostEstimate(flops=flops, bytes_accessed=nbytes, transcendentals=0),
        compiler_params=pltpu.CompilerParams(vmem_limit_bytes=limit * MIB),
    )


def pairs(x, axis, odd):
    nx, ny = lax.axis_size("gx"), lax.axis_size("gy")
    moves = []
    for u in range(nx):
        for w in range(ny):
            at, size = (u, nx) if axis == 0 else (w, ny)
            if odd and at in (0, size - 1):
                to = (u, w ^ 1) if axis == 0 else (u ^ 1, w)
            else:
                other = at + 1 if at % 2 == odd else at - 1
                to = (other, w) if axis == 0 else (u, other)
            moves.append((u * ny + w, to[0] * ny + to[1]))
    return lax.ppermute(x, ("gx", "gy"), moves)


def shards(start_block, tiles, tile_cols, node_diag, face_tiles, face_rows, filter_bounds):
    block = start_block[0, 0]
    stored = tiles[0, 0]
    cols = tile_cols[0, 0].T
    diag = node_diag[0, 0]
    coupling = face_tiles[0, 0]
    rows = face_rows[0, 0]
    count, width, tile = block.shape
    faces = rows.shape[1]
    nx, ny = lax.axis_size("gx"), lax.axis_size("gy")
    peers = nx * ny
    nodes = float(count * tile * peers)
    vec = in_vmem((count, width, tile), F32)
    vec2 = in_vmem((count, 2 * width, tile), BF16)
    vec8 = in_vmem((count, 2 * width, tile), F8)
    scale = in_vmem((width, tile), F32)
    half_face = jax.ShapeDtypeStruct((faces // 2, width, tile), F32)
    face = jax.ShapeDtypeStruct((faces, width, tile), F32)
    high, low = in_vmem(stored.shape, BF16), in_vmem(stored.shape, F8)
    face2 = in_vmem(coupling.shape, BF16)
    square = in_vmem((width, width), F32)
    small = jax.ShapeDtypeStruct((peers, 4, 128), F32)
    local_flops = 16 * stored.size * width

    rows, cols, filter_bounds, flags, ch, cl, dh, dl, block, x2, x8, undo, *sends, early = call(
        begin_kernel, "begin", [HBM] * 6,
        [
            pltpu.SMEM(rows.shape, jnp.int32), pltpu.SMEM(cols.shape, jnp.int32),
            pltpu.SMEM((2,), F32), pltpu.SMEM((6,), jnp.int32),
            face2, face2, face2, face2, vec, vec2, vec8, scale, face, face, face, face,
            in_vmem((EARLY,) + stored.shape[1:], F32),
        ],
        [pltpu.VMEM(coupling.shape, F32), pltpu.SemaphoreType.DMA((2 * (faces // CHUNK) + 6,))],
        limit=8, flops=local_flops // 2, nbytes=4 * stored.size // 2, smem=4,
    )(*(in_hbm(x) for x in (rows, cols, filter_bounds, block, coupling, stored)))

    def exchange(sends):
        return tuple(pairs(x, k // 2, k % 2) for k, x in enumerate(sends))

    received = exchange(sends)
    wf, wb, th, tl, thT, tlT = call(
        first_kernel, "local_first", [SM] + [VM] * 4 + [HBM], [vec, vec, high, low, high, low],
        [
            pltpu.VMEM((4, ROWS) + stored.shape[1:], F32),
            pltpu.SemaphoreType.DMA((4,)),
        ],
        limit=16, flops=local_flops, nbytes=4 * stored.size,
    )(cols, x2, x8, undo, early, in_hbm(stored))

    x, older = block, None
    for order in (1, 2, 3):
        carried = (x,) if older is None else (x, older)
        last = order == 3
        outs = [vec, vec2] + ([half_face] * 4 if last else [vec8, scale] + [face] * 4)
        new, new2, *sends = call(
            functools.partial(next_kernel, order), "finish%d" % order,
            [SM, SM, SM] + [VM] * (11 + len(carried)), outs,
            [pltpu.VMEM((count, width, tile), F32)],
        )(rows, flags, filter_bounds, *carried, wf, wb, diag, *received, dh, dl, ch, cl)
        x, x2, older = new, new2, x
        if not last:
            x8, undo, *sends = sends
            received = exchange(sends)
            wf, wb = call(
                local_kernel, "local%d" % (order + 1), [SM] + [VM] * 7, [vec, vec],
                flops=local_flops, nbytes=4 * stored.size,
            )(cols, x2, x8, undo, th, tl, thT, tlT)
    received = exchange(sends)
    part, over, gram = call(
        project_kernel, "project", [SM, SM] + [VM] * 5,
        [square, in_vmem((2, faces // 2, 2 * width, tile), BF16), square],
        [pltpu.VMEM((count, width, tile), F32)],
        flops=local_flops // 4, nbytes=2 * stored.size,
    )(rows, cols, x, x2, diag, th, ch)
    (sums,) = call(project_faces_kernel, "project_faces", [SM, SM] + [VM] * 8, [small])(
        rows, flags, x2, over, *received, part, gram
    )
    sums = lax.all_to_all(sums, ("gx", "gy"), 0, 0)
    basis, projected = call(
        functools.partial(end_kernel, nodes), "end", [VM, VM],
        [jax.ShapeDtypeStruct((count, width, tile), F32), jax.ShapeDtypeStruct((width, width), F32)],
        [pltpu.VMEM((count, width, tile), F32), pltpu.SemaphoreType.DMA((count // 16,))],
        out_specs=[HBM, VM],
    )(sums, x2)
    return (basis[None, None], projected)


def solution(mesh):
    in_specs = (
        P("gx", "gy", None, None, None),
        P("gx", "gy", None, None, None, None),
        P("gx", "gy", None, None),
        P("gx", "gy", None, None),
        P("gx", "gy", None, None, None, None),
        P("gx", "gy", None, None),
        P(),
    )
    out_specs = (P("gx", "gy", None, None, None), P())
    return jax.shard_map(shards, mesh=mesh, in_specs=in_specs, out_specs=out_specs, check_vma=False)
```

```python
import functools

import jax
import jax.numpy as jnp
from jax import lax
from jax.experimental import pallas as pl
from jax.experimental.pallas import tpu as pltpu
from jax.sharding import PartitionSpec as P

F32 = jnp.float32
BF16 = jnp.bfloat16
F8 = jnp.float8_e4m3fn
MIB = 1 << 20
VM = pl.BlockSpec(memory_space=pltpu.VMEM)
SM = pl.BlockSpec(memory_space=pltpu.SMEM)
HBM = pl.BlockSpec(memory_space=pltpu.HBM)
cat = jnp.concatenate

ROWS = 8
FACES = 24
WIDE = 64
CHUNK = 12
EARLY = 16
TILE_SCALE = 2.0**19
VEC_SCALE = 256.0
SHRINK = 1.0 / 64.0


def split(x):
    high = x.astype(BF16)
    low = (x - high.astype(F32)).astype(BF16)
    return high, low


def low_tile(t, high):
    return ((t - high.astype(F32)) * TILE_SCALE).astype(F8)


def stacked8(x):
    high = x.astype(F8)
    low = (x - high.astype(F32)).astype(F8)
    return cat([high, low], axis=-2)


def vector_scales(peak):
    top = jnp.maximum(jnp.max(peak, axis=1, keepdims=True), 1e-30)
    top = jnp.broadcast_to(top, peak.shape)
    return VEC_SCALE / top, top * (1.0 / (VEC_SCALE * TILE_SCALE))


def shrunk(v, v8, peak, undo):
    up, down = vector_scales(peak)
    undo[...] = down
    group = 16

    def step(s, carry):
        part = pl.ds(s * group, group)
        v8[part] = stacked8(v[part] * up)
        return carry

    lax.fori_loop(0, v.shape[0] // group, step, 0)


def stacked(x):
    return cat(split(x), axis=-2)


def dot_nn(x, t):
    return lax.dot_general(x, t, (((1,), (0,)), ((), ())), preferred_element_type=F32)


def dot_nt(x, t):
    return lax.dot_general(x, t, (((1,), (1,)), ((), ())), preferred_element_type=F32)


def fold(both, low=None):
    half = both.shape[0] // 2
    out = both[:half] + both[half:]
    return out if low is None else out + low


def two_piece(dot, x2, high, low):
    half = x2.shape[0] // 2
    return fold(dot(x2, high), dot(x2[:half], low))


def place_rows(w_ref, rows, which, data, j):
    at = rows[which, j]
    w_ref[at] = w_ref[at] + data


def leave(v, v2, rows, flags, ch, cl, sends):
    def step(s, carry):
        outs = []
        for axis in range(2):
            for r in range(FACES):
                j = s * FACES + r
                x2 = v2[rows[2 * axis, j]]
                outs.append((axis, j, two_piece(dot_nn, x2, ch[axis, j], cl[axis, j])))
        for axis, j, out in outs:
            send(rows, flags, v, axis, j, out, sends)
        return carry

    lax.fori_loop(0, rows.shape[1] // FACES, step, 0)


def begin_kernel(rows_in, cols_in, bounds_in, block, tiles, stored, *refs):
    (rows, cols, bounds, flags, ch, cl, dh, dl, v, v2, v8, undo, a, b, c, d, early, stage, sems) = refs
    faces = rows.shape[1]
    chunks = faces // CHUNK

    def fetch(s, axis):
        part = pl.ds(s * CHUNK, CHUNK)
        at = sems.at[2 * s + axis]
        return pltpu.make_async_copy(tiles.at[axis, part], stage.at[axis, part], at)

    def bring(source, target, k):
        copy = pltpu.make_async_copy(source, target, sems.at[2 * chunks + k])
        copy.start()
        return copy

    small = [bring(x, y, k) for k, (x, y) in enumerate(((rows_in, rows), (block, v)))]
    for s in range(chunks):
        for axis in range(2):
            fetch(s, axis).start()
    nx, ny = lax.axis_size("gx"), lax.axis_size("gy")
    ix, iy = lax.axis_index("gx"), lax.axis_index("gy")
    for k, flag in enumerate((ix < nx - 1, ix > 0, iy < ny - 1, iy > 0, ix % 2 == 1, iy % 2 == 1)):
        flags[k] = flag.astype(jnp.int32)
    late = [bring(cols_in, cols, 3), bring(bounds_in, bounds, 4)]
    late.append(bring(stored.at[pl.ds(0, EARLY)], early, 5))
    for copy in small:
        copy.wait()
    v2[...] = stacked(v[...])
    shrunk(v, v8, jnp.max(jnp.abs(v[...]), axis=0), undo)

    def step(s, carry):
        outs = []
        for axis in range(2):
            fetch(s, axis).wait()
            for r in range(CHUNK):
                j = s * CHUNK + r
                high, low = split(stage[axis, j])
                ch[axis, j] = high
                cl[axis, j] = low
                dh[axis, j] = high.T
                dl[axis, j] = low.T
                outs.append((axis, j, two_piece(dot_nn, v2[rows[2 * axis, j]], high, low)))
        for axis, j, out in outs:
            send(rows, flags, v, axis, j, out, (a, b, c, d))
        return carry

    lax.fori_loop(0, chunks, step, 0)
    for copy in late:
        copy.wait()


def send(rows, flags, v, axis, j, product, sends):
    minus = v[rows[2 * axis + 1, j]]
    odd = flags[4 + axis] > 0
    sends[2 * axis][j] = jnp.where(odd, minus, product)
    sends[2 * axis + 1][j] = jnp.where(odd, product, minus)


def local_rows(rows, cols, v2, v8, undo, pieces, wf, wb):
    down = undo[...]
    wide = cat([down] * 4, axis=1)
    outs = []
    for r, i in enumerate(rows):
        high, low, high_t, low_t = pieces(r, i)
        at = [cols[k, i] for k in range(4)]
        high = cat(high, axis=1)
        low = cat(low, axis=1)
        forward = fold(dot_nn(cat([v2[c] for c in at], axis=1), cat(high_t, axis=0)))
        forward = forward + down * fold(dot_nn(cat([v8[c] for c in at], axis=1), cat(low_t, axis=0)))
        backward = fold(dot_nn(v2[i], high)) + wide * fold(dot_nn(v8[i], low))
        outs.append((forward, backward))
    for i, (forward, backward) in zip(rows, outs):
        wf[i] = forward
        for k in range(4):
            at = cols[k, i]
            wb[at] = wb[at] + backward[:, k * 128 : (k + 1) * 128]


def first_kernel(cols, v2, v8, undo, early, tiles, wf, wb, th, tl, thT, tlT, stage, sems):
    copies = tiles.shape[0] // ROWS - EARLY // ROWS
    slots = stage.shape[0]
    ahead = slots - 1

    def fetch(c):
        slot = lax.rem(c, slots)
        part = pl.ds(EARLY + c * ROWS, ROWS)
        return pltpu.make_async_copy(tiles.at[part], stage.at[slot], sems.at[slot])

    for c in range(ahead):
        fetch(jnp.int32(c)).start()
    wb[...] = jnp.zeros_like(wb)

    def work(source, start):
        def pieces(r, i):
            made = [[], [], [], []]
            for k in range(4):
                t = source[r, k]
                high = t.astype(BF16)
                low = low_tile(t, high)
                for out, ref, x in zip(made, (th, tl, thT, tlT), (high, low, high.T, low.T)):
                    ref[i, k] = x
                    out.append(x)
            return made

        local_rows([start + r for r in range(ROWS)], cols, v2, v8, undo, pieces, wf, wb)

    def step_early(c, carry):
        work(early.at[pl.ds(c * ROWS, ROWS)], c * ROWS)
        return carry

    def step(c, carry):
        fetch(c).wait()

        @pl.when(c + ahead < copies)
        def _():
            fetch(c + ahead).start()

        work(stage.at[lax.rem(c, slots)], EARLY + c * ROWS)
        return carry

    lax.fori_loop(0, EARLY // ROWS, step_early, 0)
    lax.fori_loop(0, copies, step, 0)


def local_kernel(cols, v, peak, v2, th, tl, thT, tlT, wf, wb, v8, undo):
    shrunk(v, v8, peak[...], undo)
    wb[...] = jnp.zeros_like(wb)

    def step(c, carry):
        rows = [c * WIDE + r for r in range(WIDE)]

        def pieces(r, i):
            return [[ref[i, k] for k in range(4)] for ref in (th, tl, thT, tlT)]

        local_rows(rows, cols, v2, v8, undo, pieces, wf, wb)
        return carry

    lax.fori_loop(0, v2.shape[0] // WIDE, step, 0)


def arrive(rows, flags, received, dh, dl, acc):
    faces = rows.shape[1]

    def step(s, carry):
        outs = []
        for axis in range(2):
            odd = flags[4 + axis] > 0
            for r in range(FACES):
                j = s * FACES + r
                even, other = received[2 * axis][j], received[2 * axis + 1][j]
                u2 = stacked(jnp.where(flags[2 * axis] > 0, jnp.where(odd, other, even), 0.0))
                gain = two_piece(dot_nn, u2, dh[axis, j], dl[axis, j])
                outs.append((axis, j, gain, jnp.where(flags[2 * axis + 1] > 0, jnp.where(odd, even, other), 0.0)))
        for axis, j, gain, low in outs:
            place_rows(acc, rows, 2 * axis, gain, j)
            place_rows(acc, rows, 2 * axis + 1, low, j)
        return carry

    lax.fori_loop(0, faces // FACES, step, 0)


def next_kernel(order, rows, flags, bounds, *refs):
    if order == 1:
        (v, wf, wb, diag, ux, lx, uy, ly, dh, dl, ch, cl, *outs, acc) = refs
        older = None
    else:
        (v, older, wf, wb, diag, ux, lx, uy, ly, dh, dl, ch, cl, *outs, acc) = refs
    if order < 3:
        new, new2, top, *sends = outs
    else:
        new, new2, *sends = outs
    acc[...] = jnp.zeros_like(acc)
    arrive(rows, flags, (ux, lx, uy, ly), dh, dl, acc)
    lower = jnp.full((16, 128), bounds[0], F32)
    upper = jnp.full((16, 128), bounds[1], F32)
    half = (upper - lower) / 2.0
    centre = (upper + lower) / 2.0
    scale = (1.0 if order == 1 else 2.0) / half
    group = 32

    def step(s, carry):
        part = pl.ds(s * group, group)
        x = v[part]
        ax = wf[part] + wb[part] + acc[part] + diag[part][:, None, :] * x
        y = (ax - centre * x) * scale
        if older is not None:
            y = y - older[part]
        new[part] = y
        new2[part] = stacked(y)
        return jnp.maximum(carry, jnp.max(jnp.abs(y), axis=0))

    peak = lax.fori_loop(0, v.shape[0] // group, step, jnp.zeros((16, 128), F32))
    if order < 3:
        top[...] = peak
        leave(new, new2, rows, flags, ch, cl, sends)
        return
    last_sends(new, new2, rows, flags, ch, sends)


def last_sends(v, v2, rows, flags, ch, sends):
    part = rows.shape[1] // 2
    outs = []
    for axis in range(2):
        for j in range(part):
            outs.append((axis, j, fold(dot_nn(v2[rows[2 * axis, j]], ch[axis, j]))))
    for axis, j, out in outs:
        minus = v[rows[2 * axis + 1, part + j]]
        odd = flags[4 + axis] > 0
        sends[2 * axis][j] = jnp.where(odd, minus, out)
        sends[2 * axis + 1][j] = jnp.where(odd, out, minus)


def quarter(total):
    half = total.shape[0] // 2
    return (total[:half, :half] + total[half:, half:]) + (total[:half, half:] + total[half:, :half])


def spread(out, gram, half):
    n = gram.shape[0]
    value = cat([cat([x[k : k + 2] for k in range(0, n, 2)], axis=1) for x in (gram, half)], axis=0)

    def step(d, carry):
        out[d] = value
        return carry

    lax.fori_loop(0, out.shape[0], step, 0)


def project_kernel(rows, cols, v, v2, diag, th, ch, out, over, gram, wb):
    group = 8

    def begin(s, carry):
        part = pl.ds(s * group, group)
        wb[part] = 0.5 * (diag[part][:, None, :] * v[part])
        return carry

    lax.fori_loop(0, v.shape[0] // group, begin, 0)

    def step(c, carry):
        outs = []
        for r in range(WIDE):
            i = c * WIDE + r
            outs.append((i, fold(dot_nn(v2[i], cat([th[i, k] for k in range(4)], axis=1)))))
        for i, backward in outs:
            for k in range(4):
                at = cols[k, i]
                wb[at] = wb[at] + backward[:, k * 128 : (k + 1) * 128]
        return carry

    lax.fori_loop(0, v.shape[0] // WIDE, step, 0)

    part = over.shape[1]
    for axis in range(2):
        for j in range(part):
            product = fold(dot_nn(v2[rows[2 * axis, part + j]], ch[axis, part + j]))
            over[axis, j] = stacked(product * SHRINK)
    total = other = jnp.zeros((32, 32), F32)
    for s in range(0, v.shape[0], 16):
        a2 = cat([v2[s + r] for r in range(16)], axis=1)
        b2 = cat([stacked(wb[s + r] * SHRINK) for r in range(16)], axis=1)
        total = total + dot_nt(a2, b2)
        other = other + dot_nt(a2, a2)
    out[...] = quarter(total)
    gram[...] = quarter(other)


def project_faces_kernel(rows, flags, v2, over, xe, xo, ye, yo, part, gram, out):
    total = jnp.zeros((32, 32), F32)
    count = xe.shape[0]
    for axis, (even, odd) in enumerate(((xe, xo), (ye, yo))):
        swapped = flags[4 + axis] > 0
        lefts, rights = [], []
        for j in range(count):
            e, o = even[j], odd[j]
            above = jnp.where(flags[2 * axis] > 0, jnp.where(swapped, o, e), 0.0)
            below = jnp.where(flags[2 * axis + 1] > 0, jnp.where(swapped, e, o), 0.0)
            lefts += [over[axis, j], stacked(below * SHRINK)]
            rights += [stacked(above), v2[rows[2 * axis + 1, j]]]
        total = total + dot_nt(cat(lefts, axis=1), cat(rights, axis=1))
    spread(out, gram[...], part[...] + quarter(total))


def end_kernel(nodes, sums, v2, out, projected, basis, sems):
    total = sums[0]
    for d in range(1, sums.shape[0]):
        total = total + sums[d]
    n = v2.shape[1] // 2
    g, half = (
        cat([total[k : k + 2, j : j + n] for j in range(0, n * n // 2, n)], axis=0) for k in (0, 2)
    )
    g = g / nodes
    row = lax.broadcasted_iota(jnp.int32, (n, n), 0)
    col = lax.broadcasted_iota(jnp.int32, (n, n), 1)
    m = cat([g, jnp.where(row == col, 1.0, 0.0).astype(F32)], axis=1)
    row = lax.broadcasted_iota(jnp.int32, m.shape, 0)
    pivots = jnp.zeros(m.shape, F32)
    for k in range(0, n, 2):
        first = jnp.broadcast_to(m[:, k : k + 1], m.shape)
        second = jnp.broadcast_to(m[:, k + 1 : k + 2], m.shape)
        pivots = jnp.where(row == k, first, pivots)
        ratio = 1.0 / first[k : k + 1]
        step = first[k + 1 : k + 2] * ratio
        second = second - first * (second[k : k + 1] * ratio)
        pivots = jnp.where(row == k + 1, second, pivots)
        top = m[k : k + 1]
        below = m[k + 1 : k + 2] - step * top
        factor = jnp.where(row > k, first * ratio, 0.0)
        other = jnp.where(row > k + 1, second * (1.0 / second[k + 1 : k + 2]), 0.0)
        m = m - factor * top - other * below
    inv = m[:, n:] / jnp.sqrt(pivots[:, n:])
    high, low = split(inv)
    left = cat([cat([high, high], axis=1), cat([low, jnp.zeros_like(low)], axis=1)], axis=0)
    group = 16
    copies = []
    for s in range(0, v2.shape[0], group):
        part = fold(dot_nn(left, cat([v2[s + r] for r in range(group)], axis=1)))
        for r in range(group):
            basis[s + r] = part[:, r * 128 : (r + 1) * 128]
        at = pl.ds(s, group)
        copies.append(pltpu.make_async_copy(basis.at[at], out.at[at], sems.at[s // group]))
        copies[-1].start()
    exact = dict(precision=lax.Precision.HIGHEST, preferred_element_type=F32)
    raw = lax.dot_general(inv, half, (((1,), (0,)), ((), ())), **exact)
    raw = lax.dot_general(raw, inv, (((1,), (1,)), ((), ())), **exact)
    projected[...] = (raw + raw.T) * (1.0 / (SHRINK * nodes))
    for copy in copies:
        copy.wait()


def in_hbm(x):
    return pltpu.with_memory_space_constraint(x, pltpu.HBM)


def in_vmem(shape, dtype):
    return pltpu.VMEM(shape, dtype)


def call(kernel, name, specs, outs, scratch=(), limit=12, flops=0, nbytes=0, smem=0, out_specs=None):
    return pl.pallas_call(
        kernel,
        name=name,
        in_specs=specs,
        out_specs=out_specs or [SM] * smem + [VM] * (len(outs) - smem),
        out_shape=outs,
        scratch_shapes=list(scratch),
        cost_estimate=pl.CostEstimate(flops=flops, bytes_accessed=nbytes, transcendentals=0),
        compiler_params=pltpu.CompilerParams(vmem_limit_bytes=limit * MIB),
    )


def pairs(x, axis, odd):
    nx, ny = lax.axis_size("gx"), lax.axis_size("gy")
    moves = []
    for u in range(nx):
        for w in range(ny):
            at, size = (u, nx) if axis == 0 else (w, ny)
            if odd and at in (0, size - 1):
                to = (u, w ^ 1) if axis == 0 else (u ^ 1, w)
            else:
                other = at + 1 if at % 2 == odd else at - 1
                to = (other, w) if axis == 0 else (u, other)
            moves.append((u * ny + w, to[0] * ny + to[1]))
    return lax.ppermute(x, ("gx", "gy"), moves)


def shards(start_block, tiles, tile_cols, node_diag, face_tiles, face_rows, filter_bounds):
    block = start_block[0, 0]
    stored = tiles[0, 0]
    cols = tile_cols[0, 0].T
    diag = node_diag[0, 0]
    coupling = face_tiles[0, 0]
    rows = face_rows[0, 0]
    count, width, tile = block.shape
    faces = rows.shape[1]
    nx, ny = lax.axis_size("gx"), lax.axis_size("gy")
    peers = nx * ny
    nodes = float(count * tile * peers)
    vec = in_vmem((count, width, tile), F32)
    vec2 = in_vmem((count, 2 * width, tile), BF16)
    vec8 = in_vmem((count, 2 * width, tile), F8)
    scale = in_vmem((width, tile), F32)
    half_face = jax.ShapeDtypeStruct((faces // 2, width, tile), F32)
    face = jax.ShapeDtypeStruct((faces, width, tile), F32)
    high, low = in_vmem(stored.shape, BF16), in_vmem(stored.shape, F8)
    face2 = in_vmem(coupling.shape, BF16)
    square = in_vmem((width, width), F32)
    small = jax.ShapeDtypeStruct((peers, 4, 128), F32)
    local_flops = 16 * stored.size * width

    rows, cols, filter_bounds, flags, ch, cl, dh, dl, block, x2, x8, undo, *sends, early = call(
        begin_kernel, "begin", [HBM] * 6,
        [
            pltpu.SMEM(rows.shape, jnp.int32), pltpu.SMEM(cols.shape, jnp.int32),
            pltpu.SMEM((2,), F32), pltpu.SMEM((6,), jnp.int32),
            face2, face2, face2, face2, vec, vec2, vec8, scale, face, face, face, face,
            in_vmem((EARLY,) + stored.shape[1:], F32),
        ],
        [pltpu.VMEM(coupling.shape, F32), pltpu.SemaphoreType.DMA((2 * (faces // CHUNK) + 6,))],
        limit=8, flops=local_flops // 2, nbytes=4 * stored.size // 2, smem=4,
    )(*(in_hbm(x) for x in (rows, cols, filter_bounds, block, coupling, stored)))

    def exchange(sends):
        return tuple(pairs(x, k // 2, k % 2) for k, x in enumerate(sends))

    received = exchange(sends)
    wf, wb, th, tl, thT, tlT = call(
        first_kernel, "local_first", [SM] + [VM] * 4 + [HBM], [vec, vec, high, low, high, low],
        [
            pltpu.VMEM((4, ROWS) + stored.shape[1:], F32),
            pltpu.SemaphoreType.DMA((4,)),
        ],
        limit=16, flops=local_flops, nbytes=4 * stored.size,
    )(cols, x2, x8, undo, early, in_hbm(stored))

    x, older = block, None
    for order in (1, 2, 3):
        carried = (x,) if older is None else (x, older)
        last = order == 3
        outs = [vec, vec2] + ([half_face] * 4 if last else [scale] + [face] * 4)
        new, new2, *sends = call(
            functools.partial(next_kernel, order), "finish%d" % order,
            [SM, SM, SM] + [VM] * (11 + len(carried)), outs,
            [pltpu.VMEM((count, width, tile), F32)],
        )(rows, flags, filter_bounds, *carried, wf, wb, diag, *received, dh, dl, ch, cl)
        x, x2, older = new, new2, x
        if not last:
            peak, *sends = sends
            received = exchange(sends)
            wf, wb = call(
                local_kernel, "local%d" % (order + 1), [SM] + [VM] * 7, [vec, vec],
                [pltpu.VMEM((count, 2 * width, tile), F8), pltpu.VMEM((width, tile), F32)],
                flops=local_flops, nbytes=4 * stored.size,
            )(cols, x, peak, x2, th, tl, thT, tlT)
    received = exchange(sends)
    part, over, gram = call(
        project_kernel, "project", [SM, SM] + [VM] * 5,
        [square, in_vmem((2, faces // 2, 2 * width, tile), BF16), square],
        [pltpu.VMEM((count, width, tile), F32)],
        flops=local_flops // 4, nbytes=2 * stored.size,
    )(rows, cols, x, x2, diag, th, ch)
    (sums,) = call(project_faces_kernel, "project_faces", [SM, SM] + [VM] * 8, [small])(
        rows, flags, x2, over, *received, part, gram
    )
    sums = lax.all_to_all(sums, ("gx", "gy"), 0, 0)
    basis, projected = call(
        functools.partial(end_kernel, nodes), "end", [VM, VM],
        [jax.ShapeDtypeStruct((count, width, tile), F32), jax.ShapeDtypeStruct((width, width), F32)],
        [pltpu.VMEM((count, width, tile), F32), pltpu.SemaphoreType.DMA((count // 16,))],
        out_specs=[HBM, VM],
    )(sums, x2)
    return (basis[None, None], projected)


def solution(mesh):
    in_specs = (
        P("gx", "gy", None, None, None),
        P("gx", "gy", None, None, None, None),
        P("gx", "gy", None, None),
        P("gx", "gy", None, None),
        P("gx", "gy", None, None, None, None),
        P("gx", "gy", None, None),
        P(),
    )
    out_specs = (P("gx", "gy", None, None, None), P())
    return jax.shard_map(shards, mesh=mesh, in_specs=in_specs, out_specs=out_specs, check_vma=False)
```
